32 devices in a mesh: layer: 8 (over z, x), tile: 4 (over y, core).
Axes of the slice: x: 2, y: 2, z: 4, core: 2. Of those that a mesh axis runs over, the one named last changes fastest.
Arguments:
- sources: float32 [8, 2, 2, 32, 8192], P('layer', None, None, None, 'tile'), may hold values from -6 to 6
- green: float32 [8, 80, 2, 128, 128], P('layer', 'tile'), may hold values from -0.25 to 0.25
- rowcol: int32 [8, 80, 2], P('layer', 'tile'), may hold values from 0 to 63, as said below
- counts: int32 [8, 16], P('layer', 'tile'), may hold values from 1 to 5, as said below
Outputs:
- traces: float32 [8, 2, 2, 32, 8192], P('layer', None, None, None, 'tile')
The draws below stay inside these ranges and needn't reach their ends.
Inputs may be any that keep to these rules, and one draw needn't show every extreme that they name: `rowcol`: the row tile of a slot of tile device t lies in t * 16 to (t + 1) * 16 - 1; its column tile differs from its row tile by at most 4. Kind 0 has 2 or more live slots; the four counts of one tile device sum to at most 10; in every layer some tile device has 5 live slots of kind 0 and 10 live slots in all.
All inputs are finite; a program needn't handle non-finite values.
Results may differ from the reference program's by a relative error of at most 0.0003.
Values sent between devices are 32-bit elements; how exact they have to be, the bound alone decides.
No kernel may reach another device: no remote copies, remote signals or barrier semaphores. Data moves between devices by JAX's collectives and lax.ppermute only.
A program may use at most 64 MiB of HBM per device.

```python
import jax
import jax.numpy as jnp
from jax import lax

IFACE = 8192
TILE = 128
SHOTS = 32
CAP = 5
BAND = 4
TICKS = 6
LAYERS = 8
TILES = 64
TILES_DEV = 16
SLOTS = 80


def draw_rowcol(key, part):
    first_key, second_key = jax.random.split(jax.random.fold_in(key, 11))
    slot = jnp.arange(SLOTS, dtype=jnp.int32)
    owner = slot // (4 * CAP)
    first = owner * TILES_DEV
    quarter = slot % (4 * CAP)
    row = first[None, :] + jax.random.randint(first_key, (LAYERS, SLOTS), 0, TILES_DEV, dtype=jnp.int32)
    offset = jax.random.randint(second_key, (LAYERS, SLOTS), -BAND, BAND + 1, dtype=jnp.int32)
    row = jnp.where(quarter[None, :] == 0, first[None, :], row)
    row = jnp.where(quarter[None, :] == 1, first[None, :] + TILES_DEV - 1, row)
    offset = jnp.where(quarter[None, :] == 0, -BAND, offset)
    offset = jnp.where(quarter[None, :] == 1, BAND, offset)
    column = jnp.clip(row + offset, 0, TILES - 1)
    return jnp.stack([row, column], axis=-1).astype(jnp.int32)


def draw_counts(key, part):
    keys = jax.random.split(jax.random.fold_in(key, 23), 4)
    devices = SLOTS // CAP // 4
    kind_zero = jax.random.randint(keys[0], (LAYERS, devices, 1), 2, CAP + 1, dtype=jnp.int32)
    room = (2 * CAP - kind_zero) // 3
    spread = jax.random.randint(keys[1], (LAYERS, devices, 3), 0, CAP, dtype=jnp.int32)
    others = 1 + spread % room
    normal_rows = jnp.concatenate([kind_zero, others], axis=-1)
    chosen = jax.random.randint(keys[2], (LAYERS, 1, 1), 0, 3, dtype=jnp.int32)
    lanes = jnp.arange(3, dtype=jnp.int32)[None, None, :]
    busy_others = 1 + jnp.where(lanes == chosen, CAP - 3, 0)
    busy_row = jnp.concatenate([jnp.full((LAYERS, 1, 1), CAP, jnp.int32), busy_others], axis=-1)
    busiest = jax.random.randint(keys[3], (LAYERS, 1, 1), 0, devices, dtype=jnp.int32)
    device_index = jnp.arange(devices, dtype=jnp.int32)[None, :, None]
    result = jnp.where(device_index == busiest, busy_row, normal_rows)
    return result.reshape(LAYERS, 4 * devices).astype(jnp.int32)


def levels(rng, dims, shards, smallest, largest):
    def one(position, parts):
        steps = jax.random.uniform(jax.random.fold_in(jax.random.fold_in(rng, 6), position), (parts,), jnp.float32, smallest / len(shards), largest / len(shards))
        return jnp.repeat(jnp.exp(steps), dims[position] // parts).reshape((-1,) + (1,) * (len(dims) - position - 1))

    loudness = one(*shards[0])
    for cut in shards[1:]:
        loudness = loudness * one(*cut)
    return loudness


def normal_values(stream_key, shape, width, bound, cuts=(), held_as=jnp.bfloat16):
    loudness = levels(stream_key, shape, cuts, -0.22, 0.18) if cuts else 1.0
    array = jax.random.normal(stream_key, shape, jnp.float32) * width * loudness
    return jnp.minimum(jnp.maximum(array, -bound), bound).astype(held_as)


def setup_inputs(seed: int = 0) -> dict:
    arg_keys = jax.random.split(jax.random.key(seed), 5)
    sources = normal_values(arg_keys[0], (LAYERS, 2, 2, SHOTS, IFACE), 1.0, 6.0, ((0, 8), (4, 4)), jnp.float32)
    green = normal_values(arg_keys[1], (LAYERS, SLOTS, 2, TILE, TILE), (4 * TILE) ** -0.5, 0.25, ((0, 8), (1, 4)), jnp.float32)
    rowcol = draw_rowcol(jax.random.fold_in(arg_keys[4], 71), 0)
    counts = draw_counts(jax.random.fold_in(arg_keys[4], 71), 0)
    return dict(sources=sources, green=green, rowcol=rowcol, counts=counts)


def apply_layer(prev_down, next_up, blocks, pairs, live_counts):
    slot = jnp.arange(SLOTS, dtype=jnp.int32)
    group = slot // CAP
    kind = group % 4
    live = ((slot % CAP) < live_counts[group]).astype(jnp.float32)
    anchor = jnp.where((kind == 1) | (kind == 2), 1, 0).astype(jnp.int32)
    source = jnp.stack([prev_down, next_up]).reshape(2, 2, SHOTS, TILES, TILE)
    picked = source[anchor, :, :, pairs[:, 1]]
    prod = jnp.einsum('ncsj,ndij->ncdsi', picked, blocks, precision=lax.Precision.HIGHEST)
    real = prod[:, 0, 0] - prod[:, 1, 1]
    imag = prod[:, 0, 1] + prod[:, 1, 0]
    terms = jnp.stack([real, imag], axis=1) * live[:, None, None, None]
    target = (jnp.where(kind < 2, 0, 1) * TILES + pairs[:, 0]).astype(jnp.int32)
    summed = jax.ops.segment_sum(terms, target, num_segments=2 * TILES)
    summed = summed.reshape(2, TILES, 2, SHOTS, TILE).transpose(0, 2, 3, 1, 4)
    return summed.reshape(2, 2, SHOTS, IFACE)


def reference(sources, green, rowcol, counts):
    traces = jnp.zeros_like(sources)
    for sweep in range(TICKS):
        down = traces[:, 0]
        upward = traces[:, 1]
        prev_down = jnp.concatenate([jnp.zeros_like(down[:1]), down[:-1]], axis=0)
        next_up = jnp.concatenate([upward[1:], jnp.zeros_like(upward[:1])], axis=0)
        update = lax.map(lambda items: apply_layer(*items), (prev_down, next_up, green, rowcol, counts))
        traces = sources + update
    return traces
```

```python
import functools

import jax
import jax.numpy as jnp
from jax import lax
from jax.experimental import pallas as pl
from jax.experimental.pallas import tpu as pltpu
from jax.sharding import PartitionSpec as P

TILE = 128
CAP = 5
TICKS = 6
KINDS = 4
LIVE = 2 * CAP
SIDE = 2 * CAP - 2

VMEM = pl.BlockSpec(memory_space=pltpu.VMEM)
SMEM = pl.BlockSpec(memory_space=pltpu.SMEM)
LIMIT = 48 * 1024 * 1024


def partner(index, offset, count):
    return index ^ offset if count & (count - 1) == 0 else (index + offset) % count


def swap_tile(block, offset):
    count = lax.axis_size("tile")
    return lax.ppermute(block, "tile", [(i, partner(i, offset, count)) for i in range(count)])


def source_of(place, offset, count):
    return place ^ offset if count & (count - 1) == 0 else lax.rem(place - offset + count, count)


def target_of(place, offset, count):
    return place ^ offset if count & (count - 1) == 0 else lax.rem(place + offset, count)


def gather_groups(own):
    count = lax.axis_size("tile")
    groups = {0: own}
    if count & (count - 1) == 0:
        bit = count // 2
        while bit:
            for offset in list(groups):
                groups[offset ^ bit] = swap_tile(groups[offset], bit)
            bit //= 2
    else:
        for offset in range(1, count):
            groups[offset] = swap_tile(own, offset)
    return [groups[offset] for offset in range(count)]


def swap_layers(first, second):
    layers = lax.axis_size("layer")
    odd = [(i, i + 1) for i in range(1, layers - 1, 2)]
    even = [(i, i + 1) for i in range(0, layers - 1, 2)]
    both = lambda pairs: pairs + [(b, a) for a, b in pairs]
    return lax.ppermute(first, "layer", both(odd)), lax.ppermute(second, "layer", both(even))


def local_codes(pairs, live_counts):
    slot = jnp.arange(KINDS * CAP, dtype=jnp.int32)
    kind = slot // CAP
    bound = jnp.sum(jnp.where(kind[:, None] == jnp.arange(KINDS)[None, :], live_counts[None, :], 0), axis=1)
    live = slot % CAP < bound
    before = slot[None, :] < slot[:, None]
    rank = jnp.sum(jnp.where(before & live[None, :], 1, 0), axis=1)
    hot = live[:, None] & (rank[:, None] == jnp.arange(LIVE, dtype=jnp.int32)[None, :])
    code = pairs[:, 0] * 65536 + pairs[:, 1] * 8 + kind * 2 + 1
    order = jnp.sum(jnp.where(hot, slot[:, None], 0), axis=0)
    codes = jnp.sum(jnp.where(hot, code[:, None], 0), axis=0)
    return order.astype(jnp.int32), codes.astype(jnp.int32)


def lists(codes, layer, place, tiles, cap, cap_read):
    layers, devices, _ = codes.shape
    flat = codes.reshape(layers, devices * LIVE)
    alive = flat & 1
    kind = (flat >> 1) & 3
    col = (flat >> 3) & 8191
    row = flat >> 16
    wdir = kind >> 1
    rdir = (kind ^ (kind >> 1)) & 1
    tile = jnp.arange(tiles, dtype=jnp.int32)
    row_hot = (row[:, :, None] == tile) & (alive[:, :, None] == 1)
    col_hot = (col[:, :, None] == tile) & (alive[:, :, None] == 1)
    written, read = [], []
    for d in range(2):
        written.append(jnp.any(row_hot & (wdir[:, :, None] == d), axis=1))
        read.append(jnp.any(col_hot & (rdir[:, :, None] == d), axis=1))
    none = jnp.zeros((1, tiles), jnp.bool_)
    wanted = jnp.stack([jnp.concatenate([read[0][1:], none]), jnp.concatenate([none, read[1][:-1]])], axis=1)
    sent = wanted & jnp.stack(written, axis=1)
    before = (tile[:, None] < tile[None, :]).astype(jnp.int32)

    def place_in(chosen):
        return jnp.sum(jnp.where(chosen, 1, 0)[..., :, None] * before, axis=-2)

    most = jnp.max(jnp.sum(jnp.where(sent, 1, 0), axis=-1))
    odd = layer & 1

    def mine(table, shift):
        padded = jnp.concatenate([jnp.zeros_like(table[:1]), table, jnp.zeros_like(table[:1])])
        return lax.dynamic_index_in_dim(padded, layer + 1 + shift, axis=0, keepdims=False)

    sent_at = jnp.where(sent, place_in(sent) + 1, 0)
    want_at = jnp.where(wanted, place_in(wanted) + 1, 0)
    my = lambda values: lax.dynamic_index_in_dim(values, layer, axis=0, keepdims=False)
    m_row_hot, m_col_hot, m_wdir, m_rdir = my(row_hot), my(col_hot), my(wdir), my(rdir)

    def look(hot, table, side):
        rows = jnp.where(side[:, None] == 0, table[0][None], table[1][None])
        return jnp.sum(jnp.where(hot, rows, 0), axis=1)

    sent_here = mine(sent_at, 0)
    sent_in = jnp.stack([mine(sent_at, -1)[0], mine(sent_at, 1)[1]])
    want_in = jnp.stack([mine(want_at, -1)[0], mine(want_at, 1)[1]])
    send = look(m_row_hot, sent_here, m_wdir)
    recv = look(m_col_hot, sent_in, m_rdir)
    src = look(m_col_hot, want_in, m_rdir)
    send_buf = jnp.where(odd == 1, m_wdir, 1 - m_wdir)
    recv_buf = jnp.where(odd == 1, 1 - m_rdir, m_rdir)
    send = jnp.where(send > 0, send_buf * cap + send - 1, 2 * cap)
    recv = jnp.where(recv > 0, recv_buf * cap + recv - 1, 2 * cap)
    src = jnp.where(src > 0, recv_buf * cap_read + src - 1, 2 * cap_read)
    per_slot = jnp.stack([send, recv, src]).reshape(3, devices, LIVE)
    per_slot = jnp.concatenate(
        [
            lax.dynamic_index_in_dim(per_slot, source_of(place, k, devices), axis=1, keepdims=False)
            for k in range(devices)
        ],
        axis=1,
    )
    want_here = mine(want_at, 0)
    entry = jnp.arange(1, cap_read + 1, dtype=jnp.int32)
    ids = jnp.sum(jnp.where(want_here[:, None, :] == entry[None, :, None], tile, 0), axis=-1)
    first = jnp.where(odd == 1, 0, 1)
    ids = jnp.where(first == 0, jnp.stack([ids[0], ids[1]]), jnp.stack([ids[1], ids[0]]))
    dirs = jnp.stack([first, 1 - first])
    wanted_ids = jnp.concatenate([ids.reshape(-1), dirs, place[None]]).astype(jnp.int32)
    return per_slot.astype(jnp.int32), wanted_ids, most


def split_kernel(green_ref, high_ref, low_ref):
    for slot in range(green_ref.shape[0]):
        for part in range(2):
            block = green_ref[slot, part].T
            high = block.astype(jnp.bfloat16)
            low = (block - high.astype(jnp.float32)).astype(jnp.bfloat16)
            high_ref[slot, :, part * TILE : (part + 1) * TILE] = high
            low_ref[slot, :, part * TILE : (part + 1) * TILE] = low


def split_green(packed):
    shape = jax.ShapeDtypeStruct((packed.shape[0], TILE, 2 * TILE), jnp.bfloat16)
    return pl.pallas_call(
        split_kernel,
        out_shape=(shape, shape),
        in_specs=[VMEM],
        out_specs=(VMEM, VMEM),
        compiler_params=pltpu.CompilerParams(vmem_limit_bytes=LIMIT),
        name="split_green",
    )(packed)


def pick_kernel(tiles_dev, cap_read, ids_ref, *refs):
    pieces, (first_ref, second_ref) = refs[:-2], refs[-2:]
    devices = len(pieces)
    place = ids_ref[2 * cap_read + 2]
    for half, out_ref in enumerate((first_ref, second_ref)):
        direction = ids_ref[2 * cap_read + half]

        def one(j, carry):
            tile = ids_ref[half * cap_read + j]
            owner = lax.div(tile, tiles_dev)
            start = pl.multiple_of(lax.rem(tile, tiles_dev) * TILE, TILE)
            for offset in range(devices):

                @pl.when(owner == source_of(place, offset, devices))
                def _():
                    for part in range(2):
                        block = pieces[offset][direction, part, :, pl.ds(start, TILE)]
                        out_ref[j, part] = block

            return carry

        lax.fori_loop(0, cap_read, one, 0)


def pick_tiles(ids, pieces, tiles_dev, cap_read):
    sub = pieces[0].shape[2]
    shape = jax.ShapeDtypeStruct((cap_read, 2, sub, TILE), jnp.float32)
    return pl.pallas_call(
        functools.partial(pick_kernel, tiles_dev, cap_read),
        out_shape=(shape, shape),
        in_specs=[SMEM] + [VMEM] * len(pieces),
        out_specs=(VMEM, VMEM),
        compiler_params=pltpu.CompilerParams(vmem_limit_bytes=LIMIT),
        name="pick_tiles",
    )(ids, *pieces)


def either(index, first_ref, second_ref):
    cap = first_ref.shape[0]
    a = first_ref[jnp.minimum(index, cap - 1)]
    b = second_ref[jnp.clip(index - cap, 0, cap - 1)]
    zero = jnp.zeros_like(a)
    return jnp.where(index < cap, a, jnp.where(index < 2 * cap, b, zero))


def block_term(x, high, low):
    parts, sub, _ = x.shape
    flat = x.reshape(parts * sub, TILE)
    top = flat.astype(jnp.bfloat16)
    rest = (flat - top.astype(jnp.float32)).astype(jnp.bfloat16)
    rows = parts * sub
    main = jnp.dot(jnp.concatenate([top, rest], axis=0), high, preferred_element_type=jnp.float32)
    prod = main[:rows] + main[rows:] + jnp.dot(top, low, preferred_element_type=jnp.float32)
    real = prod[:sub, :TILE] - prod[sub:, TILE:]
    imag = prod[:sub, TILE:] + prod[sub:, :TILE]
    return real, imag


def tick_kernel(stage, devices, cap, idx_ref, *refs):
    refs = list(refs)
    highs = [refs.pop(0) for _ in range(devices)]
    lows = [refs.pop(0) for _ in range(devices)]
    if stage == "first":
        src_a, src_b = refs.pop(0), refs.pop(0)
        x_out = refs.pop(2)
    else:
        xs, got_a, got_b = refs.pop(0), refs.pop(0), refs.pop(0)
    if stage == "last":
        outs = refs
    else:
        out_a, out_b, acc = refs
        acc[...] = jnp.zeros_like(acc)
    for group in range(devices):
        for j in range(LIVE):
            slot = group * LIVE + j
            if stage == "first":
                x = either(idx_ref[2, slot], src_a, src_b)
                x_out[slot] = x
            else:
                x = xs[slot] + either(idx_ref[1, slot], got_a, got_b)
            real, imag = block_term(x, highs[group][j], lows[group][j])
            if stage == "last":
                outs[group][j, 0] = real
                outs[group][j, 1] = imag
            else:
                at = idx_ref[0, slot]
                acc[at, 0] += real
                acc[at, 1] += imag
    if stage != "last":
        out_a[...] = acc[:cap]
        out_b[...] = acc[cap : 2 * cap]


def tick(stage, cap, idx, highs, lows, *data):
    devices = len(highs)
    sub = data[0].shape[2]
    slots = devices * LIVE
    tile_shape = lambda count: jax.ShapeDtypeStruct((count, 2, sub, TILE), jnp.float32)
    scratch = []
    if stage == "last":
        out_shape = tuple(tile_shape(LIVE) for _ in range(devices))
    else:
        out_shape = (tile_shape(cap), tile_shape(cap))
        if stage == "first":
            out_shape += (tile_shape(slots),)
        scratch = [pltpu.VMEM((2 * cap + 1, 2, sub, TILE), jnp.float32)]
    operands = (*highs, *lows, *data)
    return pl.pallas_call(
        functools.partial(tick_kernel, stage, devices, cap),
        out_shape=out_shape,
        in_specs=[SMEM] + [VMEM] * len(operands),
        out_specs=tuple(VMEM for _ in out_shape),
        scratch_shapes=scratch,
        compiler_params=pltpu.CompilerParams(vmem_limit_bytes=LIMIT),
        name="tick_" + stage,
    )(idx, *operands)


def finish_kernel(idx_ref, sources_ref, *refs):
    out_ref = refs[-1]
    terms = refs[:-1]
    out_ref[...] = sources_ref[...]
    sub = terms[0].shape[2]
    for j in range(LIVE):
        direction = idx_ref[0, j]
        start = pl.multiple_of(idx_ref[1, j] * TILE, TILE)
        for offset, term in enumerate(terms):
            shot = pl.multiple_of(idx_ref[2, offset] * sub, sub)
            for part in range(2):
                at = (direction, part, pl.ds(shot, sub), pl.ds(start, TILE))
                out_ref[at] += term[j, part]


def finish(idx, sources, terms):
    return pl.pallas_call(
        finish_kernel,
        out_shape=jax.ShapeDtypeStruct(sources.shape, sources.dtype),
        in_specs=[SMEM] + [VMEM] * (1 + len(terms)),
        out_specs=VMEM,
        compiler_params=pltpu.CompilerParams(vmem_limit_bytes=LIMIT),
        name="finish",
    )(idx, sources, *terms)


def body(sources, green, rowcol, counts):
    devices = lax.axis_size("tile")
    layers = lax.axis_size("layer")
    layer = lax.axis_index("layer")
    place = lax.axis_index("tile")
    width = sources.shape[-1]
    shots = sources.shape[3]
    sub = shots // devices
    tiles_dev = width // TILE
    tiles = tiles_dev * devices
    local = sources[0]
    cap = SIDE * devices
    cap_read = SIDE * devices

    order, codes = local_codes(rowcol[0], counts[0])
    packed = jnp.take(green[0], order, axis=0)

    def shots_of(device):
        return lax.dynamic_slice_in_dim(local, device * sub, sub, axis=2)

    pieces = [shots_of(place)]
    for offset in range(1, devices):
        pieces.append(swap_tile(shots_of(target_of(place, offset, devices)), offset))

    groups = gather_groups(packed)
    tray = jnp.zeros((layers * devices, 1, 128), jnp.int32)
    tray = tray + jnp.pad(codes, (0, 128 - LIVE))[None, None, :]
    tray = lax.all_to_all(tray, ("layer", "tile"), 0, 0, tiled=True)
    table = tray[:, 0, :LIVE].reshape(layers, devices, LIVE)
    idx, wanted, _ = lists(table, layer, place, tiles, cap, cap_read)

    picked = pick_tiles(wanted, pieces, tiles_dev, cap_read)
    src = swap_layers(*picked)
    highs, lows = zip(*[split_green(group) for group in groups])

    out_a, out_b, xs = tick("first", cap, idx, highs, lows, *src)
    for _ in range(TICKS - 3):
        got = swap_layers(out_a, out_b)
        out_a, out_b = tick("middle", cap, idx, highs, lows, xs, *got)
    got = swap_layers(out_a, out_b)
    terms = tick("last", cap, idx, highs, lows, xs, *got)

    back = [terms[0]]
    for offset in range(1, devices):
        home = offset if devices & (devices - 1) == 0 else devices - offset
        back.append(swap_tile(terms[offset], home))
    row_local = (codes >> 16) - place * tiles_dev
    live = codes & 1
    where = jnp.zeros((3, 16), jnp.int32)
    where = where.at[0, :LIVE].set(((codes >> 1) & 3) >> 1)
    where = where.at[1, :LIVE].set(jnp.where(live == 1, row_local, 0))
    shot_groups = jnp.stack([target_of(place, k, devices) for k in range(devices)])
    where = where.at[2, :devices].set(shot_groups)
    return finish(where, local, back)[None]


def solution(mesh):
    return jax.shard_map(
        body,
        mesh=mesh,
        in_specs=(
            P("layer", None, None, None, "tile"),
            P("layer", "tile", None, None, None),
            P("layer", "tile", None),
            P("layer", "tile"),
        ),
        out_specs=P("layer", None, None, None, "tile"),
        check_vma=False,
    )
```

```python
import functools

import jax
import jax.numpy as jnp
from jax import lax
from jax.experimental import pallas as pl
from jax.experimental.pallas import tpu as pltpu
from jax.sharding import PartitionSpec as P

TILE = 128
CAP = 5
TICKS = 6
KINDS = 4
SLOTS = KINDS * CAP
LIVE = 2 * CAP
HALF = LIVE // 2
SIDE = 2 * CAP - 2
STRIDE = 16
SHORT = 12
SHORT_READ = 9
SHIFT = 1024

VMEM = pl.BlockSpec(memory_space=pltpu.VMEM)
SMEM = pl.BlockSpec(memory_space=pltpu.SMEM)
ANY = pl.BlockSpec(memory_space=pl.ANY)
PARAMS = pltpu.CompilerParams(vmem_limit_bytes=24 * 1024 * 1024)


def is_power(count):
    return count & (count - 1) == 0


def swap_tile(block, offset):
    count = lax.axis_size("tile")
    partner = (lambda i: i ^ offset) if is_power(count) else (lambda i: (i + offset) % count)
    return lax.ppermute(block, "tile", [(i, partner(i)) for i in range(count)])


def source_of(place, offset, count):
    return place ^ offset if is_power(count) else lax.rem(place - offset + count, count)


def target_of(place, offset, count):
    return place ^ offset if is_power(count) else lax.rem(place + offset, count)


def gather_groups(own):
    count = lax.axis_size("tile")
    groups = {0: own}
    if is_power(count):
        bit = count // 2
        while bit:
            for offset in list(groups):
                groups[offset ^ bit] = swap_tile(groups[offset], bit)
            bit //= 2
    else:
        for offset in range(1, count):
            groups[offset] = swap_tile(own, offset)
    return [groups[offset] for offset in range(count)]


def swap_layers(first, second):
    layers = lax.axis_size("layer")
    odd = [(i, i + 1) for i in range(1, layers - 1, 2)]
    even = [(i, i + 1) for i in range(0, layers - 1, 2)]
    both = lambda pairs: pairs + [(b, a) for a, b in pairs]
    return lax.ppermute(first, "layer", both(odd)), lax.ppermute(second, "layer", both(even))


def prepare_kernel(tiles_dev, where_ref, rowcol_ref, counts_ref, green_ref, codes_ref, rows_ref, *refs):
    halves, order_ref, sems = refs[:2], refs[2], refs[3]
    place = where_ref[1]

    def scan(want_live, rank):
        for slot in range(SLOTS):
            live = counts_ref[slot // CAP] > slot % CAP

            @pl.when((live == want_live) & (rank < LIVE))
            def _():
                order_ref[rank] = slot

            rank = rank + (live == want_live).astype(jnp.int32)
        return rank

    live_slots = scan(True, jnp.int32(0))
    scan(False, live_slots)
    copies = []
    for j in range(LIVE):
        copy = pltpu.make_async_copy(green_ref.at[order_ref[j]], halves[j // HALF].at[j % HALF], sems.at[j])
        copy.start()
        copies.append(copy)
    lanes = codes_ref.shape[-1]
    lane = lax.broadcasted_iota(jnp.int32, (1, lanes), 1)
    codes = jnp.zeros((1, lanes), jnp.int32)
    for j in range(LIVE):
        slot = order_ref[j]
        kind = lax.div(slot, CAP)
        alive = j < live_slots
        code = rowcol_ref[slot, 0] * 65536 + rowcol_ref[slot, 1] * 8 + kind * 2 + 1
        code = jnp.where(alive, code, 0)
        codes = jnp.where(lane == place * STRIDE + j, code, codes)
        rows_ref[0, j] = lax.shift_right_logical(kind, 1)
        rows_ref[1, j] = jnp.where(alive, rowcol_ref[slot, 0] - place * tiles_dev, 0)
    codes_ref[...] = jnp.broadcast_to(codes[None], codes_ref.shape)
    for copy in copies:
        copy.wait()


def prepare(where, pairs, live_counts, green, receivers, lanes, tiles_dev):
    half = jax.ShapeDtypeStruct((HALF,) + green.shape[1:], green.dtype)
    return pl.pallas_call(
        functools.partial(prepare_kernel, tiles_dev),
        out_shape=(
            jax.ShapeDtypeStruct((receivers, 1, lanes), jnp.int32),
            jax.ShapeDtypeStruct((2, STRIDE), jnp.int32),
            half,
            half,
        ),
        in_specs=[SMEM, SMEM, SMEM, ANY],
        out_specs=(VMEM, SMEM, VMEM, VMEM),
        scratch_shapes=[pltpu.SMEM((SLOTS,), jnp.int32), pltpu.SemaphoreType.DMA((LIVE,))],
        compiler_params=PARAMS,
        name="prepare",
    )(where, pairs, live_counts, green)


def lists_kernel(layers, devices, tiles_dev, where_ref, table_ref, out_ref):
    lanes = table_ref.shape[-1]
    tiles = tiles_dev * devices
    layer, place = where_ref[0], where_ref[1]
    tile = lax.broadcasted_iota(jnp.int32, (tiles, lanes), 0)
    lane = lax.broadcasted_iota(jnp.int32, (tiles, lanes), 1)

    def codes_of(index):
        total = table_ref[index * devices]
        for device in range(1, devices):
            total = total + table_ref[index * devices + device]
        return total

    def unpack(code):
        kind = (code >> 1) & 3
        return (code & 1) == 1, code >> 16, (code >> 3) & 8191, kind >> 1, (kind ^ (kind >> 1)) & 1

    def hots(code):
        alive, row, col, wdir, rdir = unpack(code)
        return (row == tile) & alive, (col == tile) & alive, wdir, rdir

    def column(hot):
        return jnp.minimum(jnp.sum(jnp.where(hot, 1.0, 0.0), axis=1, keepdims=True), 1.0)

    def columns(code):
        row_hot, col_hot, wdir, rdir = hots(code)
        return [column(h & (side == d)) for h, side in ((row_hot, wdir), (col_hot, rdir)) for d in range(2)]

    def longest(wanted):
        most = jnp.sum(wanted[:tiles_dev], axis=0, keepdims=True)
        for device in range(1, devices):
            most = jnp.maximum(
                most, jnp.sum(wanted[device * tiles_dev : (device + 1) * tiles_dev], axis=0, keepdims=True)
            )
        return most

    def one(index, carry):
        w0, w1, r0, r1, most_sent, most_read = carry
        v0, v1, q0, q1 = columns(codes_of(index))
        most_sent = jnp.maximum(most_sent, jnp.sum(w0 * q0, axis=0, keepdims=True))
        most_sent = jnp.maximum(most_sent, jnp.sum(v1 * r1, axis=0, keepdims=True))
        most_read = jnp.maximum(most_read, longest(q0))
        most_read = jnp.maximum(most_read, longest(r1))
        return v0, v1, q0, q1, most_sent, most_read

    none = jnp.zeros((1, 1), jnp.float32)
    start = (*columns(codes_of(0)), none, none)
    most_sent, most_read = lax.fori_loop(1, layers, one, start)[4:]

    has_above = layer > 0
    has_below = layer < layers - 1
    mine = codes_of(layer)
    above = jnp.where(has_above, codes_of(jnp.maximum(layer - 1, 0)), 0)
    below = jnp.where(has_below, codes_of(jnp.minimum(layer + 1, layers - 1)), 0)
    w0, w1, r0, r1 = columns(mine)
    r0 = jnp.where(has_above, r0, 0.0)
    r1 = jnp.where(has_below, r1, 0.0)
    above_w0, _, _, want_up = columns(above)
    _, below_w1, want_down, _ = columns(below)
    chosen = [w0 * want_down, w1 * want_up, above_w0 * r0, below_w1 * r1, want_down, want_up, r0, r1]
    matrix = jnp.zeros((tiles, lanes), jnp.float32)
    for j, values in enumerate(chosen):
        matrix = jnp.where(lane == j, values, matrix)
    matrix = matrix.astype(jnp.bfloat16)
    at = lax.broadcasted_iota(jnp.int32, (tiles, tiles), 0)
    other = lax.broadcasted_iota(jnp.int32, (tiles, tiles), 1)

    def group_of(index):
        total = jnp.zeros_like(index)
        for device in range(1, devices):
            total = total + jnp.where(index >= device * tiles_dev, 1, 0)
        return total

    before = other < at
    inside = before & (group_of(other) == group_of(at))
    as_mask = lambda mask: jnp.where(mask, 1.0, 0.0).astype(jnp.bfloat16)
    position = jnp.dot(as_mask(before), matrix, preferred_element_type=jnp.float32)
    position_in = jnp.dot(as_mask(inside), matrix, preferred_element_type=jnp.float32)

    def entry(j, table):
        return chosen[j] * (table[:, j : j + 1] + 1.0)

    row_hot, col_hot, wdir, rdir = hots(mine)

    def look(hot, side, down, up):
        values = jnp.where(hot, jnp.where(side == 0, down, up), 0.0)
        return jnp.sum(values, axis=0, keepdims=True).astype(jnp.int32) - 1

    odd = layer & 1
    send = look(row_hot, wdir, entry(0, position), entry(1, position))
    recv = look(col_hot, rdir, entry(2, position), entry(3, position))
    src = look(col_hot, rdir, entry(6, position_in), entry(7, position_in))
    _, _, col, _, _ = unpack(mine)
    send_buf = jnp.where(odd == 1, wdir, 1 - wdir)
    recv_buf = jnp.where(odd == 1, 1 - rdir, rdir)
    group = group_of(col)
    if is_power(devices):
        offset = group ^ place
    else:
        offset = jnp.where(group > place, place + devices - group, place - group)
    send = jnp.where(send < 0, -1, send_buf * SHIFT + send)
    recv = jnp.where(recv < 0, -1, recv_buf * SHIFT + recv)
    src = jnp.where(src < 0, -1, (offset * 2 + recv_buf) * SHIFT + src)

    own = jnp.where(group_of(tile) == place, 1.0, 0.0)

    def ids(j):
        found = jnp.where(entry(j, position_in) == (lane + 1).astype(jnp.float32), own * tile.astype(jnp.float32), 0.0)
        return jnp.sum(found, axis=0, keepdims=True).astype(jnp.int32)

    down_ids, up_ids = ids(4), ids(5)
    first = jnp.where(odd == 1, down_ids, up_ids)
    second = jnp.where(odd == 1, up_ids, down_ids)
    lane_row = lane[:1]
    facts = jnp.where(lane_row == 0, most_sent.astype(jnp.int32), most_read.astype(jnp.int32))
    facts = jnp.where(lane_row == 2, odd, facts)
    facts = jnp.where(lane_row == 3, place, facts)
    for j, values in enumerate((send, recv, src, first, second, facts)):
        out_ref[j : j + 1] = values
    out_ref[6:] = jnp.zeros((out_ref.shape[0] - 6, lanes), jnp.int32)


def build_lists(where, table, layers, devices, tiles_dev):
    return pl.pallas_call(
        functools.partial(lists_kernel, layers, devices, tiles_dev),
        out_shape=jax.ShapeDtypeStruct((8, table.shape[-1]), jnp.int32),
        in_specs=[SMEM, VMEM],
        out_specs=VMEM,
        compiler_params=PARAMS,
        name="build_lists",
    )(where, table)


def split_kernel(green_ref, high_ref, low_ref):
    for slot in range(green_ref.shape[0]):
        for part in range(2):
            block = green_ref[slot, part].T
            high = block.astype(jnp.bfloat16)
            low = (block - high.astype(jnp.float32)).astype(jnp.bfloat16)
            high_ref[slot, :, part * TILE : (part + 1) * TILE] = high
            low_ref[slot, :, part * TILE : (part + 1) * TILE] = low


def split_green(packed):
    shape = jax.ShapeDtypeStruct((packed.shape[0], TILE, 2 * TILE), jnp.bfloat16)
    return pl.pallas_call(
        split_kernel,
        out_shape=(shape, shape),
        in_specs=[VMEM],
        out_specs=(VMEM, VMEM),
        compiler_params=PARAMS,
        name="split_green",
    )(packed)


def pick_kernel(devices, lists_ref, sources_ref, *out_refs):
    sub, tiles_dev = sources_ref.shape[2] // devices, sources_ref.shape[3] // TILE
    odd, place = lists_ref[5, 2], lists_ref[5, 3]
    for half, out_ref in enumerate(out_refs):
        direction = jnp.where(odd == 1, half, 1 - half)

        def one(j, carry):
            local = jnp.maximum(lists_ref[3 + half, j] - place * tiles_dev, 0)
            start = pl.multiple_of(local * TILE, TILE)
            for offset in range(devices):
                shot = pl.multiple_of(target_of(place, offset, devices) * sub, sub)
                for part in range(2):
                    out_ref[offset, j, part] = sources_ref[direction, part, pl.ds(shot, sub), pl.ds(start, TILE)]
            return carry

        lax.fori_loop(0, out_ref.shape[1], one, 0, unroll=True)


def pick_tiles(lists, sources, devices, cap_read):
    sub = sources.shape[2] // devices
    shape = jax.ShapeDtypeStruct((devices, cap_read, 2, sub, TILE), jnp.float32)
    return pl.pallas_call(
        functools.partial(pick_kernel, devices),
        out_shape=(shape, shape),
        in_specs=[SMEM, VMEM],
        out_specs=(VMEM, VMEM),
        compiler_params=PARAMS,
        name="pick_tiles",
    )(lists, sources)


def block_term(x, high, low):
    parts, sub, _ = x.shape
    rows = parts * sub
    flat = x.reshape(rows, TILE)
    top = flat.astype(jnp.bfloat16)
    rest = (flat - top.astype(jnp.float32)).astype(jnp.bfloat16)
    main = jnp.dot(jnp.concatenate([top, rest], axis=0), high, preferred_element_type=jnp.float32)
    prod = main[:rows] + main[rows:] + jnp.dot(top, low, preferred_element_type=jnp.float32)
    real = prod[:sub, :TILE] - prod[sub:, TILE:]
    imag = prod[:sub, TILE:] + prod[sub:, :TILE]
    return real, imag


def tick_kernel(stage, devices, lists_ref, *refs):
    refs = list(refs)
    highs = [refs.pop(0) for _ in range(2 * devices)]
    lows = [refs.pop(0) for _ in range(2 * devices)]
    place = lists_ref[5, 3]

    def position(row, lane, cap, empty):
        value = lists_ref[row, lane]
        found = lax.shift_right_logical(value, 10) * cap + (value & (SHIFT - 1))
        return jnp.where(value < 0, empty, found)

    if stage == "first":
        came = [refs.pop(0) for _ in range(devices)]
        out_a, out_b, x_out, got, acc = refs
        buffers = [ref.at[half] for ref in came for half in range(2)]
    else:
        xs, came_a, came_b = refs.pop(0), refs.pop(0), refs.pop(0)
        got = refs.pop()
        buffers = [came_a, came_b]
        if stage == "middle":
            out_a, out_b, acc = refs
        else:
            outs = refs
    got_cap = buffers[0].shape[0]
    got_empty = len(buffers) * got_cap
    for j, ref in enumerate(buffers):
        got[j * got_cap : (j + 1) * got_cap] = ref[...]
    got[got_empty] = jnp.zeros(got.shape[1:], jnp.float32)
    if stage != "last":
        cap = out_a.shape[0]
        acc[...] = jnp.zeros_like(acc)
    for group in range(devices):
        base = source_of(place, group, devices) * STRIDE
        for j in range(LIVE):
            slot = group * LIVE + j
            half, row = j // HALF, j % HALF
            high, low = highs[half * devices + group][row], lows[half * devices + group][row]
            if stage == "first":
                x = got[position(2, base + j, got_cap, got_empty)]
                x_out[slot] = x
            else:
                x = xs[slot] + got[position(1, base + j, got_cap, got_empty)]
            real, imag = block_term(x, high, low)
            if stage == "last":
                outs[group][j, 0] = real
                outs[group][j, 1] = imag
            else:
                at = position(0, base + j, cap, 2 * cap)
                acc[at, 0] += real
                acc[at, 1] += imag
    if stage != "last":
        out_a[...] = acc[:cap]
        out_b[...] = acc[cap : 2 * cap]


def tick(stage, devices, cap, lists, blocks, *data):
    sub = data[0].shape[-2]
    tile_shape = lambda count: jax.ShapeDtypeStruct((count, 2, sub, TILE), jnp.float32)
    room = lambda count: pltpu.VMEM((count, 2, sub, TILE), jnp.float32)
    if stage == "first":
        got = 2 * devices * data[0].shape[1] + 1
    else:
        got = 2 * cap + 1
    if stage == "last":
        out_shape = tuple(tile_shape(LIVE) for _ in range(devices))
        scratch = [room(got)]
    else:
        out_shape = (tile_shape(cap), tile_shape(cap))
        if stage == "first":
            out_shape += (tile_shape(devices * LIVE),)
            scratch = [room(got), room(2 * cap + 1)]
        else:
            scratch = [room(2 * cap + 1), room(got)]
    operands = (*blocks, *data)
    return pl.pallas_call(
        functools.partial(tick_kernel, stage, devices),
        out_shape=out_shape,
        in_specs=[SMEM] + [VMEM] * len(operands),
        out_specs=tuple(VMEM for _ in out_shape),
        scratch_shapes=scratch,
        compiler_params=PARAMS,
        name="tick_" + stage,
    )(lists, *operands)


def finish_kernel(where_ref, rows_ref, sources_ref, *refs):
    out_ref = refs[-1]
    terms = refs[:-1]
    out_ref[...] = sources_ref[...]
    devices = len(terms)
    sub = terms[0].shape[2]
    place = where_ref[1]
    for j in range(LIVE):
        direction = rows_ref[0, j]
        start = pl.multiple_of(rows_ref[1, j] * TILE, TILE)
        for offset, term in enumerate(terms):
            shot = pl.multiple_of(target_of(place, offset, devices) * sub, sub)
            for part in range(2):
                at = (direction, part, pl.ds(shot, sub), pl.ds(start, TILE))
                out_ref[at] += term[j, part]


def finish(where, rows, sources, terms):
    return pl.pallas_call(
        finish_kernel,
        out_shape=jax.ShapeDtypeStruct(sources.shape, sources.dtype),
        in_specs=[SMEM, SMEM] + [VMEM] * (1 + len(terms)),
        out_specs=VMEM,
        compiler_params=PARAMS,
        name="finish",
    )(where, rows, sources, *terms)


def sweeps(cap, cap_read, lists, sources, early, late):
    devices = lax.axis_size("tile")
    picked = pick_tiles(lists, sources, devices, cap_read)
    first, second = swap_layers(*picked)
    late = gather_groups(late)
    came = [jnp.stack([first[0], second[0]])]
    for offset in range(1, devices):
        came.append(swap_tile(jnp.stack([first[offset], second[offset]]), offset))
    highs, lows = zip(*[split_green(group) for group in early + late])
    blocks = highs + lows
    out_a, out_b, xs = tick("first", devices, cap, lists, blocks, *came)
    for _ in range(TICKS - 3):
        out_a, out_b = tick("middle", devices, cap, lists, blocks, xs, *swap_layers(out_a, out_b))
    terms = tick("last", devices, cap, lists, blocks, xs, *swap_layers(out_a, out_b))
    back = [terms[0]]
    for offset in range(1, devices):
        back.append(swap_tile(terms[offset], offset if is_power(devices) else devices - offset))
    return tuple(back)


def body(sources, green, rowcol, counts):
    devices = lax.axis_size("tile")
    layers = lax.axis_size("layer")
    tiles_dev = sources.shape[-1] // TILE
    local = sources[0]
    lanes = -(-devices * STRIDE // 128) * 128
    where = jnp.stack([lax.axis_index("layer"), lax.axis_index("tile")]).astype(jnp.int32)

    codes, rows, early, late = prepare(
        where, rowcol[0], counts[0], green[0], layers * devices, lanes, tiles_dev
    )
    early = gather_groups(early)
    table = lax.all_to_all(codes, ("layer", "tile"), 0, 0, tiled=True)
    lists = build_lists(where, table, layers, devices, tiles_dev)
    long_lists = (SIDE * devices, tiles_dev)
    short_lists = (min(SHORT, long_lists[0]), min(SHORT_READ, long_lists[1]))
    fits = (lists[5, 0] <= short_lists[0]) & (lists[5, 1] <= short_lists[1])
    terms = lax.cond(
        fits,
        functools.partial(sweeps, *short_lists),
        functools.partial(sweeps, *long_lists),
        lists,
        local,
        early,
        late,
    )
    return finish(where, rows, local, terms)[None]


def solution(mesh):
    return jax.shard_map(
        body,
        mesh=mesh,
        in_specs=(
            P("layer", None, None, None, "tile"),
            P("layer", "tile", None, None, None),
            P("layer", "tile", None),
            P("layer", "tile"),
        ),
        out_specs=P("layer", None, None, None, "tile"),
        check_vma=False,
    )
```

```python
import functools

import jax
import jax.numpy as jnp
from jax import lax
from jax.experimental import pallas as pl
from jax.experimental.pallas import tpu as pltpu
from jax.sharding import PartitionSpec as P

TILE = 128
CAP = 5
TICKS = 6
KINDS = 4
SLOTS = KINDS * CAP
LIVE = 2 * CAP
SIDE = 2 * CAP - 2
STRIDE = 16
SHORT = 12
SHIFT = 1024

VMEM = pl.BlockSpec(memory_space=pltpu.VMEM)
SMEM = pl.BlockSpec(memory_space=pltpu.SMEM)
HBM = pl.BlockSpec(memory_space=pltpu.HBM)
PARAMS = pltpu.CompilerParams(vmem_limit_bytes=24 * 1024 * 1024)


def is_power(count):
    return count & (count - 1) == 0


def swap_tile(block, offset):
    count = lax.axis_size("tile")
    partner = (lambda i: i ^ offset) if is_power(count) else (lambda i: (i + offset) % count)
    return lax.ppermute(block, "tile", [(i, partner(i)) for i in range(count)])


def source_of(place, offset, count):
    return place ^ offset if is_power(count) else (place - offset + count) % count


def target_of(place, offset, count):
    return place ^ offset if is_power(count) else (place + offset) % count


def direct_groups(own):
    count = lax.axis_size("tile")
    if is_power(count):
        offsets = [1 << bit for bit in reversed(range(count.bit_length() - 1))]
    else:
        offsets = range(1, count)
    return {0: own, **{offset: swap_tile(own, offset) for offset in offsets}}


def all_groups(groups):
    groups = dict(groups)
    count = lax.axis_size("tile")
    for offset in sorted(range(count), key=lambda k: bin(k).count("1")):
        if offset not in groups:
            groups[offset] = swap_tile(groups[offset & (offset - 1)], offset & -offset)
    return [groups[offset] for offset in range(count)]


def swap_layers(first, second):
    layers = lax.axis_size("layer")

    def swap(block, start):
        pairs = [(i, i + 1) for i in range(start, layers - 1, 2)]
        return lax.ppermute(block, "layer", pairs + [(b, a) for a, b in pairs])

    return swap(first, 1), swap(second, 0)


def codes_kernel(tiles_dev, where_ref, rowcol_ref, counts_ref, codes_ref, rows_ref, order_ref):
    place = where_ref[1]

    def scan(want_live, rank):
        for slot in range(SLOTS):
            live = counts_ref[slot // CAP] > slot % CAP

            @pl.when((live == want_live) & (rank < LIVE))
            def _():
                order_ref[rank] = slot

            rank = rank + (live == want_live).astype(jnp.int32)
        return rank

    live_slots = scan(True, jnp.int32(0))
    scan(False, live_slots)
    lanes = codes_ref.shape[-1]
    lane = lax.broadcasted_iota(jnp.int32, (1, lanes), 1)
    codes = jnp.zeros((1, lanes), jnp.int32)
    for j in range(LIVE):
        slot = order_ref[j]
        kind = lax.div(slot, CAP)
        alive = j < live_slots
        code = rowcol_ref[slot, 0] * 65536 + rowcol_ref[slot, 1] * 8 + kind * 2 + 1
        code = jnp.where(alive, code, 0)
        codes = jnp.where(lane == place * STRIDE + j, code, codes)
        rows_ref[0, j] = lax.shift_right_logical(kind, 1)
        rows_ref[1, j] = jnp.where(alive, rowcol_ref[slot, 0] - place * tiles_dev, 0)
    codes_ref[...] = jnp.broadcast_to(codes[None], codes_ref.shape)


def slot_codes(where, pairs, live_counts, receivers, lanes, tiles_dev):
    return pl.pallas_call(
        functools.partial(codes_kernel, tiles_dev),
        out_shape=(
            jax.ShapeDtypeStruct((receivers, 1, lanes), jnp.int32),
            jax.ShapeDtypeStruct((2, STRIDE), jnp.int32),
            jax.ShapeDtypeStruct((STRIDE,), jnp.int32),
        ),
        in_specs=[SMEM, SMEM, SMEM],
        out_specs=(VMEM, SMEM, SMEM),
        compiler_params=PARAMS,
        name="slot_codes",
    )(where, pairs, live_counts)


def pack_kernel(order_ref, green_ref, packed_ref, sems):
    copies = []
    for j in range(LIVE):
        copy = pltpu.make_async_copy(green_ref.at[order_ref[j]], packed_ref.at[j], sems.at[j])
        copy.start()
        copies.append(copy)
    for copy in copies:
        copy.wait()


def pack_green(order, green):
    return pl.pallas_call(
        pack_kernel,
        out_shape=jax.ShapeDtypeStruct((LIVE,) + green.shape[1:], green.dtype),
        in_specs=[SMEM, HBM],
        out_specs=VMEM,
        scratch_shapes=[pltpu.SemaphoreType.DMA((LIVE,))],
        compiler_params=PARAMS,
        name="pack_green",
    )(order, green)


def lists_kernel(layers, devices, tiles_dev, where_ref, table_ref, out_ref):
    lanes = table_ref.shape[-1]
    tiles = tiles_dev * devices
    layer, place = where_ref[0], where_ref[1]
    tile = lax.broadcasted_iota(jnp.int32, (tiles, lanes), 0)
    lane = lax.broadcasted_iota(jnp.int32, (tiles, lanes), 1)

    def codes_of(index):
        total = table_ref[index * devices]
        for device in range(1, devices):
            total = total + table_ref[index * devices + device]
        return total

    def unpack(code):
        kind = (code >> 1) & 3
        return (code & 1) == 1, code >> 16, (code >> 3) & 8191, kind >> 1, (kind ^ (kind >> 1)) & 1

    def hots(code):
        alive, row, col, wdir, rdir = unpack(code)
        return (row == tile) & alive, (col == tile) & alive, wdir, rdir

    def column(hot):
        return jnp.minimum(jnp.sum(jnp.where(hot, 1.0, 0.0), axis=1, keepdims=True), 1.0)

    def columns(code):
        row_hot, col_hot, wdir, rdir = hots(code)
        return [column(h & (side == d)) for h, side in ((row_hot, wdir), (col_hot, rdir)) for d in range(2)]

    def one(index, carry):
        w0, w1, r0, r1, most_sent = carry
        v0, v1, q0, q1 = columns(codes_of(index))
        most_sent = jnp.maximum(most_sent, jnp.sum(w0 * q0, axis=0, keepdims=True))
        most_sent = jnp.maximum(most_sent, jnp.sum(v1 * r1, axis=0, keepdims=True))
        return v0, v1, q0, q1, most_sent

    none = jnp.zeros((1, 1), jnp.float32)
    start = (*columns(codes_of(0)), none)
    most_sent = lax.fori_loop(1, layers, one, start)[4]

    has_above = layer > 0
    has_below = layer < layers - 1
    mine = codes_of(layer)
    above = jnp.where(has_above, codes_of(jnp.maximum(layer - 1, 0)), 0)
    below = jnp.where(has_below, codes_of(jnp.minimum(layer + 1, layers - 1)), 0)
    w0, w1, r0, r1 = columns(mine)
    r0 = jnp.where(has_above, r0, 0.0)
    r1 = jnp.where(has_below, r1, 0.0)
    above_w0, _, _, want_up = columns(above)
    _, below_w1, want_down, _ = columns(below)
    chosen = [w0 * want_down, w1 * want_up, above_w0 * r0, below_w1 * r1]
    matrix = jnp.zeros((tiles, lanes), jnp.float32)
    for j, values in enumerate(chosen):
        matrix = jnp.where(lane == j, values, matrix)
    matrix = matrix.astype(jnp.bfloat16)
    at = lax.broadcasted_iota(jnp.int32, (tiles, tiles), 0)
    other = lax.broadcasted_iota(jnp.int32, (tiles, tiles), 1)

    def group_of(index):
        total = jnp.zeros_like(index)
        for device in range(1, devices):
            total = total + jnp.where(index >= device * tiles_dev, 1, 0)
        return total

    before = other < at
    before = jnp.where(before, 1.0, 0.0).astype(jnp.bfloat16)
    position = jnp.dot(before, matrix, preferred_element_type=jnp.float32)

    def entry(j):
        return chosen[j] * (position[:, j : j + 1] + 1.0)

    row_hot, col_hot, wdir, rdir = hots(mine)

    def look(hot, side, down, up):
        values = jnp.where(hot, jnp.where(side == 0, down, up), 0.0)
        return jnp.sum(values, axis=0, keepdims=True).astype(jnp.int32) - 1

    odd = layer & 1
    send = look(row_hot, wdir, entry(0), entry(1))
    recv = look(col_hot, rdir, entry(2), entry(3))
    alive, _, col, _, _ = unpack(mine)
    send_buf = jnp.where(odd == 1, wdir, 1 - wdir)
    recv_buf = jnp.where(odd == 1, 1 - rdir, rdir)
    group = group_of(col)
    if is_power(devices):
        offset = group ^ place
    else:
        offset = jnp.where(group > place, place + devices - group, place - group)
    send = jnp.where(send < 0, -1, send_buf * SHIFT + send)
    recv = jnp.where(recv < 0, -1, recv_buf * SHIFT + recv)
    src = jnp.where(alive, (offset * 2 + recv_buf) * SHIFT + col - group * tiles_dev, -1)

    lane_row = lane[:1]
    facts = jnp.where(lane_row == 0, most_sent.astype(jnp.int32), place)
    for j, values in enumerate((send, recv, src, facts)):
        out_ref[j : j + 1] = values
    out_ref[4:] = jnp.zeros((out_ref.shape[0] - 4, lanes), jnp.int32)


def build_lists(where, table, layers, devices, tiles_dev):
    return pl.pallas_call(
        functools.partial(lists_kernel, layers, devices, tiles_dev),
        out_shape=jax.ShapeDtypeStruct((8, table.shape[-1]), jnp.int32),
        in_specs=[SMEM, VMEM],
        out_specs=VMEM,
        compiler_params=PARAMS,
        name="build_lists",
    )(where, table)


def split_kernel(green_ref, high_ref, low_ref):
    for slot in range(green_ref.shape[0]):
        for part in range(2):
            block = green_ref[slot, part].T
            high = block.astype(jnp.bfloat16)
            low = (block - high.astype(jnp.float32)).astype(jnp.bfloat16)
            high_ref[slot, :, part * TILE : (part + 1) * TILE] = high
            low_ref[slot, :, part * TILE : (part + 1) * TILE] = low


def split_green(packed):
    shape = jax.ShapeDtypeStruct((packed.shape[0], TILE, 2 * TILE), jnp.bfloat16)
    return pl.pallas_call(
        split_kernel,
        out_shape=(shape, shape),
        in_specs=[VMEM],
        out_specs=(VMEM, VMEM),
        compiler_params=PARAMS,
        name="split_green",
    )(packed)


def block_term(x, high, low):
    parts, sub, _ = x.shape
    rows = parts * sub
    flat = x.reshape(rows, TILE)
    top = flat.astype(jnp.bfloat16)
    rest = (flat - top.astype(jnp.float32)).astype(jnp.bfloat16)
    main = jnp.dot(jnp.concatenate([top, rest], axis=0), high, preferred_element_type=jnp.float32)
    prod = main[:rows] + main[rows:] + jnp.dot(top, low, preferred_element_type=jnp.float32)
    real = prod[:sub, :TILE] - prod[sub:, TILE:]
    imag = prod[:sub, TILE:] + prod[sub:, :TILE]
    return real, imag


def tick_kernel(stage, devices, lists_ref, *refs):
    refs = list(refs)
    highs = [refs.pop(0) for _ in range(devices)]
    lows = [refs.pop(0) for _ in range(devices)]
    place = lists_ref[3, 1]

    def position(row, lane, cap, empty):
        value = lists_ref[row, lane]
        found = lax.shift_right_logical(value, 10) * cap + (value & (SHIFT - 1))
        return jnp.where(value < 0, empty, found)

    if stage == "first":
        came = [refs.pop(0) for _ in range(devices)]
        out_a, out_b, x_out, traces, acc = refs
        for j, ref in enumerate(came):
            traces[2 * j : 2 * j + 2] = ref[...]
    else:
        xs, came_a, came_b = refs.pop(0), refs.pop(0), refs.pop(0)
        got = refs.pop()
        if stage == "middle":
            out_a, out_b, acc = refs
        else:
            outs = refs
        got_cap = came_a.shape[0]
        got_empty = 2 * got_cap
        got[:got_cap] = came_a[...]
        got[got_cap:got_empty] = came_b[...]
        got[got_empty] = jnp.zeros(got.shape[1:], jnp.float32)
    if stage != "last":
        cap = out_a.shape[0]
        acc[...] = jnp.zeros_like(acc)
    for group in range(devices):
        base = source_of(place, group, devices) * STRIDE
        for j in range(LIVE):
            slot = group * LIVE + j
            high, low = highs[group][j], lows[group][j]
            if stage == "first":
                value = lists_ref[2, base + j]
                piece = jnp.maximum(lax.shift_right_arithmetic(value, 10), 0)
                start = pl.multiple_of(jnp.where(value < 0, 0, value & (SHIFT - 1)) * TILE, TILE)
                x = traces[piece, :, :, pl.ds(start, TILE)]
                x = jnp.where(value < 0, jnp.zeros_like(x), x)
                x_out[slot] = x
            else:
                x = xs[slot] + got[position(1, base + j, got_cap, got_empty)]
            real, imag = block_term(x, high, low)
            if stage == "last":
                outs[group][j, 0] = real
                outs[group][j, 1] = imag
            else:
                at = position(0, base + j, cap, 2 * cap)
                acc[at, 0] += real
                acc[at, 1] += imag
    if stage != "last":
        out_a[...] = acc[:cap]
        out_b[...] = acc[cap : 2 * cap]


def tick(stage, devices, cap, lists, blocks, *data):
    sub = data[-1].shape[-2]
    tile_shape = lambda count: jax.ShapeDtypeStruct((count, 2, sub, TILE), jnp.float32)
    room = lambda count: pltpu.VMEM((count, 2, sub, TILE), jnp.float32)
    if stage == "first":
        out_shape = (tile_shape(cap), tile_shape(cap), tile_shape(devices * LIVE))
        scratch = [pltpu.VMEM((2 * devices,) + data[0].shape[1:], jnp.float32), room(2 * cap + 1)]
    elif stage == "middle":
        out_shape = (tile_shape(cap), tile_shape(cap))
        scratch = [room(2 * cap + 1), room(2 * cap + 1)]
    else:
        out_shape = tuple(tile_shape(LIVE) for _ in range(devices))
        scratch = [room(2 * cap + 1)]
    operands = (*blocks, *data)
    return pl.pallas_call(
        functools.partial(tick_kernel, stage, devices),
        out_shape=out_shape,
        in_specs=[SMEM] + [VMEM] * len(operands),
        out_specs=tuple(VMEM for _ in out_shape),
        scratch_shapes=scratch,
        compiler_params=PARAMS,
        name="tick_" + stage,
    )(lists, *operands)


def finish_kernel(where_ref, rows_ref, sources_ref, *refs):
    out_ref = refs[-1]
    terms = refs[:-1]
    out_ref[...] = sources_ref[...]
    devices = len(terms)
    sub = terms[0].shape[2]
    place = where_ref[1]
    for j in range(LIVE):
        direction = rows_ref[0, j]
        start = pl.multiple_of(rows_ref[1, j] * TILE, TILE)
        for offset, term in enumerate(terms):
            shot = pl.multiple_of(target_of(place, offset, devices) * sub, sub)
            for part in range(2):
                at = (direction, part, pl.ds(shot, sub), pl.ds(start, TILE))
                out_ref[at] += term[j, part]


def finish(where, rows, sources, terms):
    return pl.pallas_call(
        finish_kernel,
        out_shape=jax.ShapeDtypeStruct(sources.shape, sources.dtype),
        in_specs=[SMEM, SMEM] + [VMEM] * (1 + len(terms)),
        out_specs=VMEM,
        compiler_params=PARAMS,
        name="finish",
    )(where, rows, sources, *terms)


def sweeps(cap, lists, came, blocks):
    devices = lax.axis_size("tile")
    out_a, out_b, xs = tick("first", devices, cap, lists, blocks, *came)
    for _ in range(TICKS - 3):
        out_a, out_b = tick("middle", devices, cap, lists, blocks, xs, *swap_layers(out_a, out_b))
    terms = tick("last", devices, cap, lists, blocks, xs, *swap_layers(out_a, out_b))
    back = [terms[0]]
    for offset in range(1, devices):
        back.append(swap_tile(terms[offset], offset if is_power(devices) else devices - offset))
    return tuple(back)


def body(sources, green, rowcol, counts):
    devices = lax.axis_size("tile")
    layers = lax.axis_size("layer")
    tiles_dev = sources.shape[-1] // TILE
    local = sources[0]
    lanes = -(-devices * STRIDE // 128) * 128
    where = jnp.stack([lax.axis_index("layer"), lax.axis_index("tile")]).astype(jnp.int32)

    codes, rows, order = slot_codes(where, rowcol[0], counts[0], layers * devices, lanes, tiles_dev)
    groups = direct_groups(pack_green(order, green[0]))
    layer, place = lax.axis_index("layer"), lax.axis_index("tile")
    near = swap_layers(
        lax.dynamic_index_in_dim(local, 1 - layer % 2, keepdims=False),
        lax.dynamic_index_in_dim(local, layer % 2, keepdims=False),
    )
    table = lax.all_to_all(codes, ("layer", "tile"), 0, 0, tiled=True)
    near, groups, table = lax.optimization_barrier((near, groups, table))
    sub = local.shape[2] // devices

    def shots_of(offset):
        shot = target_of(place, offset, devices) * sub
        return jnp.stack([lax.dynamic_slice_in_dim(block, shot, sub, axis=1) for block in near])

    came = [shots_of(0)] + [swap_tile(shots_of(offset), offset) for offset in range(1, devices)]
    groups = all_groups(groups)
    lists = build_lists(where, table, layers, devices, tiles_dev)
    highs, lows = zip(*[split_green(group) for group in groups])
    cap = SIDE * devices
    short = min(SHORT, cap)
    terms = lax.cond(
        lists[3, 0] <= short,
        functools.partial(sweeps, short),
        functools.partial(sweeps, cap),
        lists,
        came,
        highs + lows,
    )
    return finish(where, rows, local, terms)[None]


def solution(mesh):
    return jax.shard_map(
        body,
        mesh=mesh,
        in_specs=(
            P("layer", None, None, None, "tile"),
            P("layer", "tile", None, None, None),
            P("layer", "tile", None),
            P("layer", "tile"),
        ),
        out_specs=P("layer", None, None, None, "tile"),
        check_vma=False,
    )
```

```python
import functools

import jax
import jax.numpy as jnp
from jax import lax
from jax.experimental import pallas as pl
from jax.experimental.pallas import tpu as pltpu
from jax.sharding import PartitionSpec as P

TILE = 128
CAP = 5
BAND = 4
TICKS = 6
KINDS = 4
SLOTS = KINDS * CAP
LIVE = 2 * CAP
STRIDE = 16
READ = 9
CROSS = 4
EXTRA = 4
ROUNDS = (8, 5, 4, 3)
SHIFT = 1024

VMEM = pl.BlockSpec(memory_space=pltpu.VMEM)
SMEM = pl.BlockSpec(memory_space=pltpu.SMEM)
ANY = pl.BlockSpec(memory_space=pl.ANY)
PARAMS = pltpu.CompilerParams(vmem_limit_bytes=32 * 1024 * 1024)

SEND, RECV, SOURCE, FOREIGN, OFFER, READS, LEND, COPY_OUT, COPY_IN, CODE, FACTS = 0, 4, 8, 9, 10, 11, 12, 13, 14, 15, 16
TABLE_ROWS = 24


def from_behind(block, axis, distance):
    devices = range(lax.axis_size(axis))
    route = [(i - distance, i) for i in devices if i - distance in devices]
    return lax.ppermute(block, axis, route)


def padded(cells, sides, width):
    for axis, dim in sides:
        count = lax.axis_size(axis)
        ends = count - 1
        head = lax.slice_in_dim(cells, 0, width, axis=dim)
        tail = lax.slice_in_dim(cells, cells.shape[dim] - width, cells.shape[dim], axis=dim)
        cells = jnp.concatenate(
            [
                lax.ppermute(tail, axis, [(i, (i + 1) % count) for i in range(ends)]),
                cells,
                lax.ppermute(head, axis, [((i + 1) % count, i) for i in range(ends)]),
            ],
            axis=dim,
        )
    return cells


def complex_term(picked, blocks, pattern):
    prod = jnp.einsum(pattern, picked, blocks, precision=lax.Precision.HIGHEST)
    return jnp.stack([prod[0, 0] - prod[1, 1], prod[0, 1] + prod[1, 0]])


def place_terms(terms, target, live, tiles_dev):
    onehot = (
        (target[:, None] == jnp.arange(2 * tiles_dev, dtype=jnp.int32)[None, :]) & live[:, None]
    ).astype(jnp.float32)
    onehot = onehot.reshape(target.shape[0], 2, tiles_dev)
    return jnp.einsum("csni,ngr->gcsri", terms, onehot, precision=lax.Precision.HIGHEST)


def live_update(tiled, blocks, row_local, col_local, live_counts, tiles_dev):
    slot = jnp.arange(4 * CAP, dtype=jnp.int32)
    group = slot // CAP
    live = slot % CAP < live_counts[group]
    score = jnp.where(live, 0, 4 * CAP).astype(jnp.int32) + slot
    order = jnp.argsort(score)[: 2 * CAP]
    kinds = group[order]
    anchor = jnp.where((kinds == 1) | (kinds == 2), 1, 0).astype(jnp.int32)
    picked = tiled[anchor, :, :, col_local[order]]
    chosen_blocks = jnp.take(blocks, order, axis=0)
    terms = complex_term(picked, chosen_blocks, "ncsj,ndij->cdsni")
    target = jnp.where(kinds < 2, 0, 1) * tiles_dev + row_local[order]
    return place_terms(terms, target, live[order], tiles_dev)


def full_sweeps(sources, green, rowcol, counts):
    width = sources.shape[-1]
    shots = sources.shape[3]
    tiles_dev = width // TILE
    place = lax.axis_index("tile")
    blocks = green[0]
    pairs = rowcol[0]
    live_counts = counts[0]
    row_local = pairs[:, 0] - place * tiles_dev
    col_local = pairs[:, 1] - place * tiles_dev + BAND
    local_sources = sources[0]
    waves = local_sources
    for sweep in range(TICKS - 1):
        prev_down = from_behind(waves[0], "layer", 1)
        next_up = from_behind(waves[1], "layer", -1)
        incoming = jnp.stack([prev_down, next_up])
        widened = padded(incoming, (("tile", 3),), BAND * TILE)
        tiled = widened.reshape(2, 2, shots, tiles_dev + 2 * BAND, TILE)
        update = live_update(tiled, blocks, row_local, col_local, live_counts, tiles_dev)
        waves = local_sources + update.reshape(2, 2, shots, width)
    return waves


def swap_tile(block, offset):
    return lax.ppermute(block, "tile", [(i, i ^ offset) for i in range(lax.axis_size("tile"))])


def swap_layers(first, second):
    layers = lax.axis_size("layer")

    def swap(block, start):
        pairs = [(i, i + 1) for i in range(start, layers - 1, 2)]
        return lax.ppermute(block, "layer", pairs + [(b, a) for a, b in pairs])

    return swap(first, 1), swap(second, 0)


def codes_kernel(tiles_dev, where_ref, rowcol_ref, counts_ref, codes_ref, rows_ref, order_ref):
    place = where_ref[1]

    def scan(want_live, rank):
        for slot in range(SLOTS):
            live = counts_ref[slot // CAP] > slot % CAP

            @pl.when((live == want_live) & (rank < LIVE))
            def _():
                order_ref[rank] = slot

            rank = rank + (live == want_live).astype(jnp.int32)
        return rank

    live_slots = scan(True, jnp.int32(0))
    scan(False, live_slots)
    lanes = codes_ref.shape[-1]
    lane = lax.broadcasted_iota(jnp.int32, (1, lanes), 1)
    codes = jnp.zeros((1, lanes), jnp.int32)
    for j in range(LIVE):
        slot = order_ref[j]
        kind = lax.div(slot, CAP)
        alive = j < live_slots
        code = rowcol_ref[slot, 0] * 65536 + rowcol_ref[slot, 1] * 8 + kind * 2 + 1
        code = jnp.where(alive, code, 0)
        codes = jnp.where(lane == place * STRIDE + j, code, codes)
        rows_ref[0, j] = lax.shift_right_logical(kind, 1)
        rows_ref[1, j] = jnp.where(alive, rowcol_ref[slot, 0] - place * tiles_dev, 0)
    codes_ref[...] = jnp.broadcast_to(codes[None], codes_ref.shape)


def slot_codes(where, pairs, live_counts, receivers, lanes, tiles_dev):
    return pl.pallas_call(
        functools.partial(codes_kernel, tiles_dev),
        out_shape=(
            jax.ShapeDtypeStruct((receivers, 1, lanes), jnp.int32),
            jax.ShapeDtypeStruct((2, STRIDE), jnp.int32),
            jax.ShapeDtypeStruct((STRIDE,), jnp.int32),
        ),
        in_specs=[SMEM, SMEM, SMEM],
        out_specs=(VMEM, SMEM, SMEM),
        compiler_params=PARAMS,
        name="slot_codes",
    )(where, pairs, live_counts)


def pack_kernel(order_ref, green_ref, packed_ref, sems):
    copies = []
    for j in range(LIVE):
        copy = pltpu.make_async_copy(green_ref.at[order_ref[j]], packed_ref.at[j], sems.at[j])
        copy.start()
        copies.append(copy)
    for copy in copies:
        copy.wait()


def pack_green(order, green):
    return pl.pallas_call(
        pack_kernel,
        out_shape=jax.ShapeDtypeStruct((LIVE,) + green.shape[1:], green.dtype),
        in_specs=[SMEM, ANY],
        out_specs=VMEM,
        scratch_shapes=[pltpu.SemaphoreType.DMA((LIVE,))],
        compiler_params=PARAMS,
        name="pack_green",
    )(order, green)


def lists_kernel(layers, devices, tiles_dev, where_ref, table_ref, out_ref, writes, reads, active, changed, now, sets, seen):
    lanes = 128
    tiles = tiles_dev * devices
    pad = 2
    layer, place = where_ref[0], where_ref[1]
    pair = place >> 1
    down = lax.broadcasted_iota(jnp.int32, (lanes, lanes), 0)
    across = lax.broadcasted_iota(jnp.int32, (lanes, lanes), 1)
    row8 = lax.broadcasted_iota(jnp.int32, (8, lanes), 0)
    lane8 = lax.broadcasted_iota(jnp.int32, (8, lanes), 1)
    lane = lane8[:1]
    low = lane8 < tiles
    as_mask = lambda mask: jnp.where(mask, 1.0, 0.0).astype(jnp.bfloat16)
    narrow = lambda values: values.astype(jnp.bfloat16)

    def by_rows(values, matrix):
        return lax.dot_general(narrow(values), matrix, (((1,), (1,)), ((), ())), preferred_element_type=jnp.float32)

    def by_columns(values, matrix):
        return jnp.dot(narrow(values), matrix, preferred_element_type=jnp.float32)

    def each(step):
        if layers <= 8:
            for index in range(layers):
                step(index)
        else:
            lax.fori_loop(0, layers, lambda index, carry: (step(index), carry)[1], 0)

    def code_of(index):
        total = table_ref[index * devices]
        for device in range(1, devices):
            total = total + table_ref[index * devices + device]
        return total

    for ref in (changed, now, seen):
        ref[...] = jnp.zeros_like(ref)

    def unpack(index):
        code = code_of(index)
        kind = (code >> 1) & 3
        alive = (code & 1) == 1
        wdir, rdir = kind >> 1, (kind ^ (kind >> 1)) & 1
        target = jnp.where(alive, wdir * tiles + (code >> 16), -1)
        origin = rdir * tiles + ((code >> 3) & 8191)
        from_edge = ((rdir == 0) & (index == 0)) | ((rdir == 1) & (index == layers - 1))
        origin = jnp.where(alive & jnp.logical_not(from_edge), origin, -1)
        writes[index] = as_mask(down == target)
        reads[index] = as_mask(down == origin)
        live = jnp.where(alive, 1.0, 0.0)
        active[index] = jnp.where(row8 == 0, live, 0.0)
        device = lane >> 4
        first = jnp.where((device >> 1) == 0, live, 0.0)
        second = jnp.where((device >> 1) == 1, live, 0.0)
        sets[index] = jnp.where(row8 == 0, first, jnp.where(row8 == 1, second, jnp.where(row8 == 2, live, 0.0)))

    each(unpack)

    for step in range(len(ROUNDS) + 1):
        last = step == len(ROUNDS)

        def spread(index):
            if not last:
                hit = jnp.minimum(by_rows(active[index], writes[index]), 1.0)
                now[index + pad] = hit
                changed[index + pad] = jnp.where(row8 == step, hit[:1], changed[index + pad])
            seen[index + pad] = jnp.minimum(by_rows(sets[index], reads[index]), 1.0)

        each(spread)
        if last:
            break

        def collect(index):
            coming = jnp.where(low, now[index + pad - 1], now[index + pad + 1])
            active[index] = jnp.minimum(by_columns(coming, reads[index]), 1.0)
            wanted = jnp.where(low, seen[index + pad + 1], seen[index + pad - 1])
            added = jnp.minimum(by_columns(wanted, writes[index]), 1.0)
            sets[index] = jnp.maximum(sets[index], added)

        each(collect)

    same_half = (down >= tiles) == (across >= tiles)
    same_group = (down >> 4) == (across >> 4)
    half_total, group_total = as_mask(same_half), as_mask(same_group)
    half_before = as_mask(same_half & (down < across))
    group_before = as_mask(same_group & (down < across))
    room = jnp.zeros((8, lanes), jnp.float32)
    for j, most in enumerate(ROUNDS):
        room = jnp.where(row8 == j, float(most), room)

    tile_pair = ((lane8 & (tiles - 1)) >> 4) >> 1
    slot_pair = (lane8 >> 4) >> 1

    def pick(rows, which):
        return jnp.where(which == 0, rows[0:1], rows[1:2])

    def wanted_by(which, index):
        ahead, behind = seen[index + pad + 1], seen[index + pad - 1]
        return jnp.where(low[:1], pick(ahead, which), pick(behind, which))

    now[0] = jnp.full((8, lanes), -1.0, jnp.float32)

    def measure(index):
        over = now[0]
        for which in range(2):
            counts = by_columns(changed[index + pad] * wanted_by(which, index), half_total)
            over = jnp.maximum(over, jnp.where(row8 < len(ROUNDS), counts - room, -1.0))
        counts = by_columns(seen[index + pad], group_total)
        over = jnp.maximum(over, jnp.where(row8 == 2, counts - READ, -1.0))
        over = jnp.maximum(over, jnp.where((row8 < 2) & (tile_pair != row8), counts - CROSS, -1.0))
        counts = by_columns(sets[index], group_total)
        over = jnp.maximum(over, jnp.where((row8 < 2) & (slot_pair != row8) & (slot_pair < 2), counts - EXTRA, -1.0))
        now[0] = over

    each(measure)
    over = jnp.max(jnp.max(now[0], axis=1, keepdims=True), axis=0, keepdims=True)

    odd = layer & 1
    other = 1 - pair
    code = code_of(layer)
    kind = (code >> 1) & 3
    wdir, rdir = kind >> 1, (kind ^ (kind >> 1)) & 1

    def travelling(index):
        sent = changed[index + pad] * wanted_by(pair, index)
        return sent * (by_columns(sent, half_before) + 1.0)

    def ranked(flags):
        return flags * (by_columns(flags, group_before) + 1.0)

    mine = travelling(layer)
    above = travelling(jnp.maximum(layer - 1, 0))
    below = travelling(jnp.minimum(layer + 1, layers - 1))
    coming = jnp.where(low, jnp.where(layer > 0, above, 0.0), jnp.where(layer < layers - 1, below, 0.0))
    send = by_columns(mine, writes[layer]).astype(jnp.int32) - 1
    recv = by_columns(coming, reads[layer]).astype(jnp.int32) - 1
    send = jnp.where((send >= 0) & (wdir == odd), send + SHIFT, send)
    recv = jnp.where((recv >= 0) & (rdir != odd), recv + SHIFT, recv)
    here = seen[layer + pad]
    ahead, behind = seen[layer + pad + 1], seen[layer + pad - 1]
    foreign = pick(here, pair) * jnp.where(tile_pair[:1] != pair, 1.0, 0.0)
    lent = pick(here, other)
    offered = jnp.where(low[:1], ahead[2:3], behind[2:3])
    flags = jnp.where(row8 == 0, here[2:3], 0.0)
    flags = jnp.where(row8 == 1, foreign, flags)
    flags = jnp.where(row8 == 2, offered, flags)
    flags = jnp.where(row8 == 3, lent, flags)
    ranks = ranked(flags)
    sources = by_columns(ranks, reads[layer]).astype(jnp.int32) - 1
    chosen = sets[layer]
    flags = jnp.where(row8 == 0, pick(chosen, other), 0.0)
    flags = jnp.where(row8 == 1, pick(chosen, pair) * jnp.where(slot_pair[:1] != pair, 1.0, 0.0), flags)
    copies = ranked(flags).astype(jnp.int32)
    ranks = ranks.astype(jnp.int32)
    out_ref[...] = jnp.zeros_like(out_ref)
    rounds = len(ROUNDS)
    out_ref[SEND : SEND + rounds] = send[:rounds]
    out_ref[RECV : RECV + rounds] = recv[:rounds]
    out_ref[SOURCE : SOURCE + 2] = sources[:2]
    out_ref[OFFER : OFFER + 1] = ranks[2:3]
    out_ref[READS : READS + 1] = ranks[0:1]
    out_ref[LEND : LEND + 1] = ranks[3:4]
    out_ref[COPY_OUT : COPY_OUT + 2] = copies[:2]
    out_ref[CODE : CODE + 1] = code
    facts = jnp.where(lane == 0, jnp.where(over > 0.0, 1, 0), jnp.where(lane == 1, layer, place))
    out_ref[FACTS : FACTS + 1] = facts


def build_lists(where, table, layers, devices, tiles_dev):
    lanes = table.shape[-1]
    rows = lambda count: pltpu.VMEM((count, 8, lanes), jnp.float32)
    square = pltpu.VMEM((layers, lanes, lanes), jnp.bfloat16)
    return pl.pallas_call(
        functools.partial(lists_kernel, layers, devices, tiles_dev),
        out_shape=jax.ShapeDtypeStruct((TABLE_ROWS, lanes), jnp.int32),
        in_specs=[SMEM, VMEM],
        out_specs=VMEM,
        scratch_shapes=[square, square, rows(layers), rows(layers + 4), rows(layers + 4), rows(layers), rows(layers + 4)],
        compiler_params=PARAMS,
        name="build_lists",
    )(where, table)


def split_kernel(green_ref, high_ref, low_ref):
    for slot in range(green_ref.shape[0]):
        for part in range(2):
            block = green_ref[slot, part].T
            high = block.astype(jnp.bfloat16)
            low = (block - high.astype(jnp.float32)).astype(jnp.bfloat16)
            high_ref[slot, :, part * TILE : (part + 1) * TILE] = high
            low_ref[slot, :, part * TILE : (part + 1) * TILE] = low


def split_green(packed):
    shape = jax.ShapeDtypeStruct((packed.shape[0], TILE, 2 * TILE), jnp.bfloat16)
    return pl.pallas_call(
        split_kernel,
        out_shape=(shape, shape),
        in_specs=[VMEM],
        out_specs=(VMEM, VMEM),
        compiler_params=PARAMS,
        name="split_green",
    )(packed)


def pick_kernel(tiles, lists_ref, sources_ref, packed_ref, first_ref, second_ref, copy_ref):
    odd, place = lists_ref[FACTS, 1] & 1, lists_ref[FACTS, 2]
    tiles_dev = sources_ref.shape[3] // TILE
    first_ref[...] = jnp.zeros_like(first_ref)
    second_ref[...] = jnp.zeros_like(second_ref)
    for direction in range(2):
        for tile in range(tiles_dev):
            rank = lists_ref[OFFER, direction * tiles + place * tiles_dev + tile]
            found = (rank > 0) & (rank <= READ)

            def copy_to(ref):
                ref[jnp.clip(rank - 1, 0, READ - 1)] = sources_ref[direction, :, :, tile * TILE : (tile + 1) * TILE]

            pl.when(found & (odd != direction))(functools.partial(copy_to, first_ref))
            pl.when(found & (odd == direction))(functools.partial(copy_to, second_ref))
    for j in range(LIVE):
        rank = lists_ref[COPY_OUT, place * STRIDE + j]

        @pl.when((rank > 0) & (rank <= EXTRA))
        def _():
            copy_ref[jnp.clip(rank - 1, 0, EXTRA - 1)] = packed_ref[j]


def pick_tiles(lists, sources, packed, tiles):
    shots = sources.shape[2]
    shape = jax.ShapeDtypeStruct((READ, 2, shots, TILE), jnp.float32)
    return pl.pallas_call(
        functools.partial(pick_kernel, tiles),
        out_shape=(shape, shape, jax.ShapeDtypeStruct((EXTRA,) + packed.shape[1:], packed.dtype)),
        in_specs=[SMEM, VMEM, VMEM],
        out_specs=(VMEM, VMEM, VMEM),
        compiler_params=PARAMS,
        name="pick_tiles",
    )(lists, sources, packed)


def share_kernel(tiles, tiles_dev, lists_ref, first_ref, second_ref, core_ref, *cross_refs):
    odd, place = lists_ref[FACTS, 1] & 1, lists_ref[FACTS, 2]
    sub = core_ref.shape[3]
    core = place & 1
    theirs = pl.multiple_of((1 - core) * sub, sub)
    core_ref[0] = first_ref[:, :, pl.ds(theirs, sub), :]
    core_ref[1] = second_ref[:, :, pl.ds(theirs, sub), :]
    for cross_ref in cross_refs:
        cross_ref[...] = jnp.zeros_like(cross_ref)
    for direction in range(2):
        for tile in range(tiles_dev):
            lane = direction * tiles + place * tiles_dev + tile
            rank = lists_ref[LEND, lane]
            at = jnp.clip(lists_ref[READS, lane] - 1, 0, READ - 1)

            def copy_from(ref):
                for flip, cross_ref in enumerate(cross_refs):
                    shot = pl.multiple_of((core ^ flip) * sub, sub)
                    cross_ref[direction, jnp.clip(rank - 1, 0, CROSS - 1)] = ref[at, :, pl.ds(shot, sub), :]

            found = (rank > 0) & (rank <= CROSS)
            pl.when(found & (odd == direction))(functools.partial(copy_from, first_ref))
            pl.when(found & (odd != direction))(functools.partial(copy_from, second_ref))


def share_tiles(lists, first, second, tiles, tiles_dev):
    sub = first.shape[2] // 2
    piece = jax.ShapeDtypeStruct((2, READ, 2, sub, TILE), jnp.float32)
    cross = jax.ShapeDtypeStruct((2, CROSS, 2, sub, TILE), jnp.float32)
    return pl.pallas_call(
        functools.partial(share_kernel, tiles, tiles_dev),
        out_shape=(piece, cross, cross),
        in_specs=[SMEM, VMEM, VMEM],
        out_specs=(VMEM, VMEM, VMEM),
        compiler_params=PARAMS,
        name="share_tiles",
    )(lists, first, second)


def block_term(x, high, low):
    parts, sub, _ = x.shape
    rows = parts * sub
    flat = x.reshape(rows, TILE)
    top = flat.astype(jnp.bfloat16)
    rest = (flat - top.astype(jnp.float32)).astype(jnp.bfloat16)
    main = jnp.dot(jnp.concatenate([top, rest], axis=0), high, preferred_element_type=jnp.float32)
    prod = main[:rows] + main[rows:] + jnp.dot(top, low, preferred_element_type=jnp.float32)
    real = prod[:sub, :TILE] - prod[sub:, TILE:]
    imag = prod[:sub, TILE:] + prod[sub:, :TILE]
    return real, imag


def tick_kernel(step, tiles_dev, lists_ref, *refs):
    refs = list(refs)
    highs = [refs.pop(0) for _ in range(4)]
    lows = [refs.pop(0) for _ in range(4)]
    first_ref, second_ref = refs.pop(0), refs.pop(0)
    last = step == len(ROUNDS)
    if step == 0:
        core_ref, cross_refs, (total_ref, out_a, out_b, traces, acc) = refs[0], refs[1:3], refs[3:]
    elif last:
        _, total_ref = refs
    else:
        _, total_ref, out_a, out_b, acc = refs
    odd, place = lists_ref[FACTS, 1] & 1, lists_ref[FACTS, 2]
    core = place & 1
    if step == 0:
        sub = core_ref.shape[3]
        shot = pl.multiple_of(core * sub, sub)
        traces[:READ] = first_ref[:, :, pl.ds(shot, sub), :]
        traces[READ : 2 * READ] = second_ref[:, :, pl.ds(shot, sub), :]
        traces[2 * READ : 3 * READ] = core_ref[0]
        traces[3 * READ : 4 * READ] = core_ref[1]
        for j, ref in enumerate(cross_refs):
            for direction in range(2):
                at = 4 * READ + (2 * j + direction) * CROSS
                traces[at : at + CROSS] = ref[direction]
        empty = 4 * READ + 4 * CROSS
        traces[empty] = jnp.zeros(traces.shape[1:], jnp.float32)
    if not last:
        cap = out_a.shape[0]
        acc[...] = jnp.zeros_like(acc)

    def entering(lane):
        if step:
            value = lists_ref[RECV + step - 1, lane]
            at = value & (SHIFT - 1)
            return jnp.where(value < SHIFT, first_ref[at], second_ref[at])
        code = lists_ref[CODE, lane]
        kind = lax.shift_right_logical(code, 1) & 3
        rdir = (kind ^ lax.shift_right_logical(kind, 1)) & 1
        group = lax.div(lax.shift_right_logical(code, 3) & 8191, tiles_dev)
        relative = group ^ place
        near = lists_ref[SOURCE, lane]
        far = lists_ref[FOREIGN, lane]
        near_at = relative * 2 * READ + jnp.where(rdir == odd, 0, READ) + near
        far_at = 4 * READ + (2 * (relative - 2) + rdir) * CROSS + far
        at = jnp.where(relative < 2, jnp.where(near < 0, empty, near_at), jnp.where(far < 0, empty, far_at))
        return traces[jnp.clip(at, 0, empty)]

    def apply(lane, group, row, slot):
        real, imag = block_term(entering(lane), highs[group][row], lows[group][row])
        if slot is not None:
            if step == 0:
                total_ref[slot, 0] = real
                total_ref[slot, 1] = imag
            else:
                total_ref[slot, 0] += real
                total_ref[slot, 1] += imag
        if not last:
            value = lists_ref[SEND + step, lane]
            at = jnp.where(value < SHIFT, value, value - SHIFT + cap)
            at = jnp.where(value < 0, 2 * cap, at)
            acc[at, 0] += real
            acc[at, 1] += imag

    for group in range(2):
        base = (place ^ group) * STRIDE
        for j in range(LIVE):
            step_in = functools.partial(apply, base + j, group, j, group * LIVE + j)
            if step == 0:
                step_in()
            else:
                pl.when(lists_ref[RECV + step - 1, base + j] >= 0)(step_in)
    if not last:
        for group in range(2, 4):
            base = (place ^ group) * STRIDE
            for j in range(LIVE):
                rank = lists_ref[COPY_IN, base + j]
                wanted = rank > 0
                if step:
                    wanted = wanted & (lists_ref[RECV + step - 1, base + j] >= 0)
                row = jnp.clip(rank - 1, 0, EXTRA - 1)
                pl.when(wanted)(functools.partial(apply, base + j, group, row, None))
        out_a[...] = acc[:cap]
        out_b[...] = acc[cap : 2 * cap]


def tick(step, tiles_dev, lists, blocks, first, second, *data):
    sub = data[0].shape[-2]
    tile_shape = lambda count: jax.ShapeDtypeStruct((count, 2, sub, TILE), jnp.float32)
    room = lambda count: pltpu.VMEM((count, 2, sub, TILE), jnp.float32)
    out_shape = (tile_shape(2 * LIVE),)
    scratch = []
    aliases = {}
    if step == 0:
        scratch.append(room(4 * READ + 4 * CROSS + 1))
    else:
        aliases = {1 + len(blocks) + 2: 0}
    if step < len(ROUNDS):
        cap = ROUNDS[step]
        out_shape += (tile_shape(cap), tile_shape(cap))
        scratch.append(room(2 * cap + 1))
    operands = (*blocks, first, second, *data)
    return pl.pallas_call(
        functools.partial(tick_kernel, step, tiles_dev),
        out_shape=out_shape,
        in_specs=[SMEM] + [VMEM] * len(operands),
        out_specs=tuple(VMEM for _ in out_shape),
        scratch_shapes=scratch,
        input_output_aliases=aliases,
        compiler_params=PARAMS,
        name=f"tick_{step}",
    )(lists, *operands)


def finish_kernel(where_ref, rows_ref, sources_ref, total_ref, back_ref, out_ref):
    out_ref[...] = sources_ref[...]
    sub = total_ref.shape[2]
    core = where_ref[1] & 1
    for j in range(LIVE):
        direction = rows_ref[0, j]
        start = pl.multiple_of(rows_ref[1, j] * TILE, TILE)
        for flip, ref in enumerate((total_ref, back_ref)):
            shot = pl.multiple_of((core ^ flip) * sub, sub)
            for part in range(2):
                out_ref[direction, part, pl.ds(shot, sub), pl.ds(start, TILE)] += ref[j, part]


def finish(where, rows, sources, total, back):
    return pl.pallas_call(
        finish_kernel,
        out_shape=jax.ShapeDtypeStruct(sources.shape, sources.dtype),
        in_specs=[SMEM, SMEM, VMEM, VMEM, VMEM],
        out_specs=VMEM,
        compiler_params=PARAMS,
        name="finish",
    )(where, rows, sources, total, back)


def short_sweeps(where, rows, sources, lists, blocks, near, pieces, *unused):
    tiles_dev = sources.shape[-1] // TILE
    total, out_a, out_b = tick(0, tiles_dev, lists, blocks, *near, *pieces)
    for step in range(1, len(ROUNDS) + 1):
        got = swap_layers(out_a, out_b)
        total, *out = tick(step, tiles_dev, lists, blocks, *got, total)
        if out:
            out_a, out_b = out
    back = swap_tile(total[LIVE:], 1)
    return finish(where, rows, sources, total, back)


def long_sweeps(where, rows, sources, lists, blocks, near, pieces, green, rowcol, counts):
    return full_sweeps(sources[None], green, rowcol, counts)


def body(sources, green, rowcol, counts):
    devices = lax.axis_size("tile")
    layers = lax.axis_size("layer")
    tiles_dev = sources.shape[-1] // TILE
    tiles = tiles_dev * devices
    if devices != 4 or 2 * tiles != 128 or tiles_dev != STRIDE:
        return full_sweeps(sources, green, rowcol, counts)[None]
    local = sources[0]
    where = jnp.stack([lax.axis_index("layer"), lax.axis_index("tile")]).astype(jnp.int32)

    codes, rows, order = slot_codes(where, rowcol[0], counts[0], layers * devices, 2 * tiles, tiles_dev)
    packed = pack_green(order, green[0])
    table = lax.all_to_all(codes, ("layer", "tile"), 0, 0, tiled=True)
    lists = build_lists(where, table, layers, devices, tiles_dev)
    first, second, copies = pick_tiles(lists, local, packed, tiles)
    near = swap_layers(first, second)
    partner = swap_tile(packed, 1)
    copies = swap_tile(copies, 2)
    copies_partner = swap_tile(copies, 1)
    core, *cross = share_tiles(lists, *near, tiles, tiles_dev)
    pieces = (swap_tile(core, 1), swap_tile(cross[0], 2), swap_tile(cross[1], 3))
    highs, lows = zip(*[split_green(group) for group in (packed, partner, copies, copies_partner)])
    out = lax.cond(
        lists[FACTS, 0] == 0,
        short_sweeps,
        long_sweeps,
        where,
        rows,
        local,
        lists,
        highs + lows,
        near,
        pieces,
        green,
        rowcol,
        counts,
    )
    return out[None]


def solution(mesh):
    return jax.shard_map(
        body,
        mesh=mesh,
        in_specs=(
            P("layer", None, None, None, "tile"),
            P("layer", "tile", None, None, None),
            P("layer", "tile", None),
            P("layer", "tile"),
        ),
        out_specs=P("layer", None, None, None, "tile"),
        check_vma=False,
    )
```

```python
import functools

import jax
import jax.numpy as jnp
from jax import lax
from jax.experimental import pallas as pl
from jax.experimental.pallas import tpu as pltpu
from jax.sharding import PartitionSpec as P

TILE = 128
CAP = 5
BAND = 4
TICKS = 6
KINDS = 4
SLOTS = KINDS * CAP
LIVE = 2 * CAP
STRIDE = 16
READ = 15
CROSS = 4
EXTRA = 4
ROUNDS = (8, 5, 4, 3)
SHIFT = 1024

VMEM = pl.BlockSpec(memory_space=pltpu.VMEM)
SMEM = pl.BlockSpec(memory_space=pltpu.SMEM)
ANY = pl.BlockSpec(memory_space=pl.ANY)
HBM = pl.BlockSpec(memory_space=pltpu.HBM)
PARAMS = pltpu.CompilerParams(vmem_limit_bytes=16 * 1024 * 1024)

LEND, COPY_OUT, FACTS = range(3)
SEND, RECV, COPY_IN, CODE, SOURCE, FOREIGN, STEP_FACTS = range(7)


def from_behind(block, axis, distance):
    devices = range(lax.axis_size(axis))
    route = [(i - distance, i) for i in devices if i - distance in devices]
    return lax.ppermute(block, axis, route)


def padded(cells, sides, width):
    for axis, dim in sides:
        count = lax.axis_size(axis)
        ends = count - 1
        head = lax.slice_in_dim(cells, 0, width, axis=dim)
        tail = lax.slice_in_dim(cells, cells.shape[dim] - width, cells.shape[dim], axis=dim)
        cells = jnp.concatenate(
            [
                lax.ppermute(tail, axis, [(i, (i + 1) % count) for i in range(ends)]),
                cells,
                lax.ppermute(head, axis, [((i + 1) % count, i) for i in range(ends)]),
            ],
            axis=dim,
        )
    return cells


def complex_term(picked, blocks, pattern):
    prod = jnp.einsum(pattern, picked, blocks, precision=lax.Precision.HIGHEST)
    return jnp.stack([prod[0, 0] - prod[1, 1], prod[0, 1] + prod[1, 0]])


def place_terms(terms, target, live, tiles_dev):
    onehot = (
        (target[:, None] == jnp.arange(2 * tiles_dev, dtype=jnp.int32)[None, :]) & live[:, None]
    ).astype(jnp.float32)
    onehot = onehot.reshape(target.shape[0], 2, tiles_dev)
    return jnp.einsum("csni,ngr->gcsri", terms, onehot, precision=lax.Precision.HIGHEST)


def live_update(tiled, blocks, row_local, col_local, live_counts, tiles_dev):
    slot = jnp.arange(4 * CAP, dtype=jnp.int32)
    group = slot // CAP
    live = slot % CAP < live_counts[group]
    score = jnp.where(live, 0, 4 * CAP).astype(jnp.int32) + slot
    order = jnp.argsort(score)[: 2 * CAP]
    kinds = group[order]
    anchor = jnp.where((kinds == 1) | (kinds == 2), 1, 0).astype(jnp.int32)
    picked = tiled[anchor, :, :, col_local[order]]
    chosen_blocks = jnp.take(blocks, order, axis=0)
    terms = complex_term(picked, chosen_blocks, "ncsj,ndij->cdsni")
    target = jnp.where(kinds < 2, 0, 1) * tiles_dev + row_local[order]
    return place_terms(terms, target, live[order], tiles_dev)


def full_sweeps(sources, green, rowcol, counts):
    width = sources.shape[-1]
    shots = sources.shape[3]
    tiles_dev = width // TILE
    place = lax.axis_index("tile")
    blocks = green[0]
    pairs = rowcol[0]
    live_counts = counts[0]
    row_local = pairs[:, 0] - place * tiles_dev
    col_local = pairs[:, 1] - place * tiles_dev + BAND
    local_sources = sources[0]
    waves = local_sources
    for sweep in range(TICKS - 1):
        prev_down = from_behind(waves[0], "layer", 1)
        next_up = from_behind(waves[1], "layer", -1)
        incoming = jnp.stack([prev_down, next_up])
        widened = padded(incoming, (("tile", 3),), BAND * TILE)
        tiled = widened.reshape(2, 2, shots, tiles_dev + 2 * BAND, TILE)
        update = live_update(tiled, blocks, row_local, col_local, live_counts, tiles_dev)
        waves = local_sources + update.reshape(2, 2, shots, width)
    return waves


def swap_tile(block, offset):
    return lax.ppermute(block, "tile", [(i, i ^ offset) for i in range(lax.axis_size("tile"))])


def swap_layers(first, second):
    layers = lax.axis_size("layer")

    def swap(block, start):
        pairs = [(i, i + 1) for i in range(start, layers - 1, 2)]
        return lax.ppermute(block, "layer", pairs + [(b, a) for a, b in pairs])

    return swap(first, 1), swap(second, 0)


def codes_kernel(tiles_dev, where_ref, rowcol_ref, counts_ref, codes_ref, rows_ref, order_ref):
    place = where_ref[1]

    def scan(want_live, rank):
        for slot in range(SLOTS):
            live = counts_ref[slot // CAP] > slot % CAP

            @pl.when((live == want_live) & (rank < LIVE))
            def _():
                order_ref[rank] = slot

            rank = rank + (live == want_live).astype(jnp.int32)
        return rank

    live_slots = scan(True, jnp.int32(0))
    scan(False, live_slots)
    lanes = codes_ref.shape[-1]
    lane = lax.broadcasted_iota(jnp.int32, (1, lanes), 1)
    codes = jnp.zeros((1, lanes), jnp.int32)
    for j in range(LIVE):
        slot = order_ref[j]
        kind = lax.div(slot, CAP)
        alive = j < live_slots
        code = rowcol_ref[slot, 0] * 65536 + rowcol_ref[slot, 1] * 8 + kind * 2 + 1
        code = jnp.where(alive, code, 0)
        codes = jnp.where(lane == place * STRIDE + j, code, codes)
        rows_ref[0, j] = lax.shift_right_logical(kind, 1)
        rows_ref[1, j] = jnp.where(alive, rowcol_ref[slot, 0] - place * tiles_dev, 0)
    codes_ref[...] = jnp.broadcast_to(codes[None], codes_ref.shape)


def slot_codes(where, pairs, live_counts, receivers, lanes, tiles_dev):
    return pl.pallas_call(
        functools.partial(codes_kernel, tiles_dev),
        out_shape=(
            jax.ShapeDtypeStruct((receivers, 1, lanes), jnp.int32),
            jax.ShapeDtypeStruct((2, STRIDE), jnp.int32),
            jax.ShapeDtypeStruct((STRIDE,), jnp.int32),
        ),
        in_specs=[SMEM, SMEM, SMEM],
        out_specs=(VMEM, SMEM, SMEM),
        compiler_params=PARAMS,
        name="slot_codes",
    )(where, pairs, live_counts)


def pack_kernel(order_ref, green_ref, packed_ref, sems):
    copies = []
    for j in range(LIVE):
        copy = pltpu.make_async_copy(green_ref.at[order_ref[j]], packed_ref.at[j], sems.at[j])
        copy.start()
        copies.append(copy)
    for copy in copies:
        copy.wait()


def pack_green(order, green):
    return pl.pallas_call(
        pack_kernel,
        out_shape=jax.ShapeDtypeStruct((LIVE,) + green.shape[1:], green.dtype),
        in_specs=[SMEM, ANY],
        out_specs=VMEM,
        scratch_shapes=[pltpu.SemaphoreType.DMA((LIVE,))],
        compiler_params=PARAMS,
        name="pack_green",
    )(order, green)


def lists_kernel(layers, devices, tiles_dev, where_ref, table_ref, share_ref, *refs):
    step_refs, (writes, reads, active, changed, now, sets, seen) = refs[:-7], refs[-7:]
    lanes = 128
    tiles = tiles_dev * devices
    pad = 2
    layer, place = where_ref[0], where_ref[1]
    pair = place >> 1
    down = lax.broadcasted_iota(jnp.int32, (lanes, lanes), 0)
    across = lax.broadcasted_iota(jnp.int32, (lanes, lanes), 1)
    row8 = lax.broadcasted_iota(jnp.int32, (8, lanes), 0)
    lane8 = lax.broadcasted_iota(jnp.int32, (8, lanes), 1)
    lane = lane8[:1]
    low = lane8 < tiles
    as_mask = lambda mask: jnp.where(mask, 1.0, 0.0).astype(jnp.bfloat16)
    narrow = lambda values: values.astype(jnp.bfloat16)

    def by_rows(values, matrix):
        return lax.dot_general(narrow(values), matrix, (((1,), (1,)), ((), ())), preferred_element_type=jnp.float32)

    def by_columns(values, matrix):
        return jnp.dot(narrow(values), matrix, preferred_element_type=jnp.float32)

    def each(step):
        if layers <= 8:
            for index in range(layers):
                step(index)
        else:
            lax.fori_loop(0, layers, lambda index, carry: (step(index), carry)[1], 0)

    def code_of(index):
        total = table_ref[index * devices]
        for device in range(1, devices):
            total = total + table_ref[index * devices + device]
        return total

    for ref in (changed, now, seen):
        ref[...] = jnp.zeros_like(ref)

    def unpack(index):
        code = code_of(index)
        kind = (code >> 1) & 3
        alive = (code & 1) == 1
        wdir, rdir = kind >> 1, (kind ^ (kind >> 1)) & 1
        target = jnp.where(alive, wdir * tiles + (code >> 16), -1)
        origin = rdir * tiles + ((code >> 3) & 8191)
        from_edge = ((rdir == 0) & (index == 0)) | ((rdir == 1) & (index == layers - 1))
        origin = jnp.where(alive & jnp.logical_not(from_edge), origin, -1)
        writes[index] = as_mask(down == target)
        reads[index] = as_mask(down == origin)
        live = jnp.where(alive, 1.0, 0.0)
        active[index] = jnp.where(row8 == 0, live, 0.0)
        device = lane >> 4
        first = jnp.where((device >> 1) == 0, live, 0.0)
        second = jnp.where((device >> 1) == 1, live, 0.0)
        sets[index] = jnp.where(row8 == 0, first, jnp.where(row8 == 1, second, jnp.where(row8 == 2, live, 0.0)))

    each(unpack)

    for step in range(len(ROUNDS) + 1):
        last = step == len(ROUNDS)

        def spread(index):
            if not last:
                hit = jnp.minimum(by_rows(active[index], writes[index]), 1.0)
                now[index + pad] = hit
                changed[index + pad] = jnp.where(row8 == step, hit[:1], changed[index + pad])
            seen[index + pad] = jnp.minimum(by_rows(sets[index], reads[index]), 1.0)

        each(spread)
        if last:
            break

        def collect(index):
            coming = jnp.where(low, now[index + pad - 1], now[index + pad + 1])
            active[index] = jnp.minimum(by_columns(coming, reads[index]), 1.0)
            wanted = jnp.where(low, seen[index + pad + 1], seen[index + pad - 1])
            added = jnp.minimum(by_columns(wanted, writes[index]), 1.0)
            sets[index] = jnp.maximum(sets[index], added)

        each(collect)

    same_half = (down >= tiles) == (across >= tiles)
    same_pair = (down >> 5) == (across >> 5)
    half_total, pair_total = as_mask(same_half), as_mask(same_pair)
    half_before = as_mask(same_half & (down < across))
    pair_before = as_mask(same_pair & (down < across))
    room = jnp.zeros((8, lanes), jnp.float32)
    for j, most in enumerate(ROUNDS):
        room = jnp.where(row8 == j, float(most), room)

    tile_pair = ((lane8 & (tiles - 1)) >> 4) >> 1
    slot_pair = (lane8 >> 4) >> 1

    def pick(rows, which):
        return jnp.where(which == 0, rows[0:1], rows[1:2])

    def wanted_by(which, index):
        ahead, behind = seen[index + pad + 1], seen[index + pad - 1]
        return jnp.where(low[:1], pick(ahead, which), pick(behind, which))

    now[0] = jnp.full((8, lanes), -1.0, jnp.float32)

    def measure(index):
        over = now[0]
        for which in range(2):
            counts = by_columns(changed[index + pad] * wanted_by(which, index), half_total)
            over = jnp.maximum(over, jnp.where(row8 < len(ROUNDS), counts - room, -1.0))
        counts = by_columns(seen[index + pad], pair_total)
        over = jnp.maximum(over, jnp.where(row8 == 2, counts - READ, -1.0))
        over = jnp.maximum(over, jnp.where((row8 < 2) & (tile_pair != row8), counts - CROSS, -1.0))
        counts = by_columns(sets[index], pair_total)
        over = jnp.maximum(over, jnp.where((row8 < 2) & (slot_pair != row8) & (slot_pair < 2), counts - EXTRA, -1.0))
        now[0] = over

    each(measure)
    over = jnp.max(jnp.max(now[0], axis=1, keepdims=True), axis=0, keepdims=True)

    odd = layer & 1
    other = 1 - pair
    code = code_of(layer)
    kind = (code >> 1) & 3
    wdir, rdir = kind >> 1, (kind ^ (kind >> 1)) & 1

    def travelling(index):
        sent = changed[index + pad] * wanted_by(pair, index)
        return sent * (by_columns(sent, half_before) + 1.0)

    def ranked(flags):
        return flags * (by_columns(flags, pair_before) + 1.0)

    mine = travelling(layer)
    above = travelling(jnp.maximum(layer - 1, 0))
    below = travelling(jnp.minimum(layer + 1, layers - 1))
    coming = jnp.where(low, jnp.where(layer > 0, above, 0.0), jnp.where(layer < layers - 1, below, 0.0))
    send = by_columns(mine, writes[layer]).astype(jnp.int32) - 1
    recv = by_columns(coming, reads[layer]).astype(jnp.int32) - 1
    send = jnp.where((send >= 0) & (wdir == odd), send + SHIFT, send)
    recv = jnp.where((recv >= 0) & (rdir != odd), recv + SHIFT, recv)
    here = seen[layer + pad]
    foreign = pick(here, pair) * jnp.where(tile_pair[:1] != pair, 1.0, 0.0)
    lent = pick(here, other)
    flags = jnp.where(row8 == 0, here[2:3], 0.0)
    flags = jnp.where(row8 == 1, foreign, flags)
    flags = jnp.where(row8 == 2, lent, flags)
    ranks = ranked(flags)
    sources = by_columns(ranks, reads[layer]).astype(jnp.int32) - 1
    chosen = sets[layer]
    flags = jnp.where(row8 == 0, pick(chosen, other), 0.0)
    flags = jnp.where(row8 == 1, pick(chosen, pair) * jnp.where(slot_pair[:1] != pair, 1.0, 0.0), flags)
    copies = ranked(flags).astype(jnp.int32)
    ranks = ranks.astype(jnp.int32)
    facts = jnp.where(lane == 0, jnp.where(over > 0.0, 1, 0), jnp.where(lane == 1, layer, place))

    def write(ref, rows):
        ref[...] = jnp.zeros_like(ref)
        for j, values in rows.items():
            ref[j : j + 1] = values

    lend_rank = jnp.where(tile_pair[:1] == pair, ranks[2:3], 0)
    chosen = (lend_rank == (down & (tiles - 1)) + 1) & ((across >= tiles) == (down >= tiles))
    read_at = jnp.where(chosen, (ranks[0:1] - 1).astype(jnp.float32), 0.0)
    lend = by_rows(jnp.ones((8, lanes), jnp.float32), narrow(read_at)).astype(jnp.int32)
    write(share_ref, {LEND: lend[0:1], COPY_OUT: copies[0:1], FACTS: facts})
    for step, ref in enumerate(step_refs):
        rows = {COPY_IN: copies[1:2], STEP_FACTS: facts}
        if step < len(ROUNDS):
            rows[SEND] = send[step : step + 1]
        if step:
            rows[RECV] = recv[step - 1 : step]
        else:
            rows.update({CODE: code, SOURCE: sources[0:1], FOREIGN: sources[1:2]})
        write(ref, rows)


def build_lists(where, table, layers, devices, tiles_dev):
    lanes = table.shape[-1]
    rows = lambda count: pltpu.VMEM((count, 8, lanes), jnp.float32)
    square = pltpu.VMEM((layers, lanes, lanes), jnp.bfloat16)
    return pl.pallas_call(
        functools.partial(lists_kernel, layers, devices, tiles_dev),
        out_shape=(jax.ShapeDtypeStruct((8, lanes), jnp.int32),) * (len(ROUNDS) + 2),
        in_specs=[SMEM, VMEM],
        out_specs=(VMEM,) * (len(ROUNDS) + 2),
        scratch_shapes=[square, square, rows(layers), rows(layers + 4), rows(layers + 4), rows(layers), rows(layers + 4)],
        compiler_params=PARAMS,
        name="build_lists",
    )(where, table)


def split_kernel(green_ref, high_ref, low_ref):
    for slot in range(green_ref.shape[0]):
        for part in range(2):
            block = green_ref[slot, part].T
            high = block.astype(jnp.bfloat16)
            low = (block - high.astype(jnp.float32)).astype(jnp.bfloat16)
            high_ref[slot, :, part * TILE : (part + 1) * TILE] = high
            low_ref[slot, :, part * TILE : (part + 1) * TILE] = low


def split_green(packed):
    shape = jax.ShapeDtypeStruct((packed.shape[0], TILE, 2 * TILE), jnp.bfloat16)
    return pl.pallas_call(
        split_kernel,
        out_shape=(shape, shape),
        in_specs=[VMEM],
        out_specs=(VMEM, VMEM),
        compiler_params=PARAMS,
        name="split_green",
    )(packed)


def pick_kernel(layers, devices, tiles_dev, where_ref, table_ref, own_ref, partner_ref, first_ref, second_ref, ranks, scalars, sem):
    lanes = table_ref.shape[-1]
    tiles = tiles_dev * devices
    layer, place = where_ref[0], where_ref[1]
    odd = layer & 1
    down = lax.broadcasted_iota(jnp.int32, (lanes, lanes), 0)
    across = lax.broadcasted_iota(jnp.int32, (lanes, lanes), 1)
    as_mask = lambda mask: jnp.where(mask, 1.0, 0.0).astype(jnp.bfloat16)

    def offered(index, direction):
        at = jnp.clip(index, 0, layers - 1)
        code = table_ref[at * devices]
        for device in range(1, devices):
            code = code + table_ref[at * devices + device]
        kind = (code >> 1) & 3
        rdir = (kind ^ (kind >> 1)) & 1
        live = ((code & 1) == 1) & (rdir == direction) & (index == at)
        reads = as_mask(down == jnp.where(live, direction * tiles + ((code >> 3) & 8191), -1))
        ones = jnp.ones((8, lanes), jnp.bfloat16)
        total = lax.dot_general(ones, reads, (((1,), (1,)), ((), ())), preferred_element_type=jnp.float32)
        return jnp.minimum(total, 1.0)

    flags = offered(layer + 1, 0) + offered(layer - 1, 1)
    before = as_mask(((down >> 5) == (across >> 5)) & (down < across))
    position = jnp.dot(flags.astype(jnp.bfloat16), before, preferred_element_type=jnp.float32)
    lane = across[:1]
    in_pair = ((lane & (tiles - 1)) >> 5) == (place >> 1)
    rank = jnp.where(in_pair, (flags * (position + 1.0))[:1], 0.0).astype(jnp.int32)
    chosen = (rank == (down & (tiles - 1)) + 1) & ((across >= tiles) == (down >= tiles))
    tile_of = jnp.where(chosen, (across & (tiles - 1)).astype(jnp.float32), 0.0).astype(jnp.bfloat16)
    ones = jnp.ones((8, lanes), jnp.bfloat16)
    ids = lax.dot_general(ones, tile_of, (((1,), (1,)), ((), ())), preferred_element_type=jnp.float32)
    ranks[...] = ids.astype(jnp.int32)
    copy = pltpu.make_async_copy(ranks, scalars, sem)
    copy.start()
    copy.wait()
    for j in range(READ):
        found = []
        for direction in range(2):
            tile = scalars[0, direction * tiles + j]
            start = pl.multiple_of((tile & (tiles_dev - 1)) * TILE, TILE)
            mine = ((tile // tiles_dev) ^ place) & 1 == 0
            at = (direction, slice(None), slice(None), pl.ds(start, TILE))
            found.append(jnp.where(mine, own_ref[at], partner_ref[at]))
        first_ref[j] = jnp.where(odd == 1, found[0], found[1])
        second_ref[j] = jnp.where(odd == 1, found[1], found[0])


def pick_tiles(where, table, own, partner, layers, devices, tiles_dev):
    shape = jax.ShapeDtypeStruct((READ, 2, own.shape[2], TILE), jnp.float32)
    lanes = table.shape[-1]
    return pl.pallas_call(
        functools.partial(pick_kernel, layers, devices, tiles_dev),
        out_shape=(shape, shape),
        in_specs=[SMEM, VMEM, VMEM, VMEM],
        out_specs=(VMEM, VMEM),
        scratch_shapes=[
            pltpu.VMEM((8, lanes), jnp.int32),
            pltpu.SMEM((8, lanes), jnp.int32),
            pltpu.SemaphoreType.DMA,
        ],
        compiler_params=PARAMS,
        name="pick_tiles",
    )(where, table, own, partner)


def lend_kernel(share_ref, packed_ref, partner_ref, *copy_refs):
    place = share_ref[FACTS, 2]
    half = len(copy_refs)
    for copy_ref in copy_refs:
        copy_ref[...] = jnp.zeros_like(copy_ref)
    for group, ref in enumerate((packed_ref, partner_ref)):
        for j in range(LIVE):
            rank = share_ref[COPY_OUT, (place ^ group) * STRIDE + j]
            at = rank - 1 - (place & 1) * half
            for k, copy_ref in enumerate(copy_refs):

                @pl.when((rank > 0) & (at == k))
                def _():
                    copy_ref[...] = ref[j]


def lend_blocks(share, packed, partner):
    return pl.pallas_call(
        lend_kernel,
        out_shape=(jax.ShapeDtypeStruct(packed.shape[1:], packed.dtype),) * (EXTRA // 2),
        in_specs=[SMEM, VMEM, VMEM],
        out_specs=(VMEM,) * (EXTRA // 2),
        compiler_params=PARAMS,
        name="lend_blocks",
    )(share, packed, partner)


def share_kernel(tiles, share_ref, first_ref, second_ref, cross_ref):
    odd = share_ref[FACTS, 1] & 1
    for direction in range(2):
        for j in range(CROSS):
            at = jnp.clip(share_ref[LEND, direction * tiles + j], 0, READ - 1)
            cross_ref[direction, j] = jnp.where(odd == direction, first_ref[at], second_ref[at])


def share_tiles(share, first, second, tiles):
    return pl.pallas_call(
        functools.partial(share_kernel, tiles),
        out_shape=jax.ShapeDtypeStruct((2, CROSS) + first.shape[1:], jnp.float32),
        in_specs=[SMEM, VMEM, VMEM],
        out_specs=VMEM,
        compiler_params=PARAMS,
        name="share_tiles",
    )(share, first, second)


def block_term(x, high, low):
    parts, sub, _ = x.shape
    rows = parts * sub
    flat = x.reshape(rows, TILE)
    top = flat.astype(jnp.bfloat16)
    rest = (flat - top.astype(jnp.float32)).astype(jnp.bfloat16)
    main = jnp.dot(jnp.concatenate([top, rest], axis=0), high, preferred_element_type=jnp.float32)
    prod = main[:rows] + main[rows:] + jnp.dot(top, low, preferred_element_type=jnp.float32)
    real = prod[:sub, :TILE] - prod[sub:, TILE:]
    imag = prod[:sub, TILE:] + prod[sub:, :TILE]
    return real, imag


def tick_kernel(step, tiles_dev, table_ref, *refs):
    refs = list(refs)
    highs = [refs.pop(0) for _ in range(3)]
    lows = [refs.pop(0) for _ in range(3)]
    first_ref, second_ref = refs.pop(0), refs.pop(0)
    last = step == len(ROUNDS)
    if step == 0:
        cross_ref, total_ref, out_a, out_b, traces, acc = refs
    elif last:
        _, total_ref = refs
    else:
        _, total_ref, out_a, out_b, acc = refs
    odd, place = table_ref[STEP_FACTS, 1] & 1, table_ref[STEP_FACTS, 2]
    core = place & 1
    if step == 0:
        traces[:READ] = first_ref[...]
        traces[READ : 2 * READ] = second_ref[...]
        for direction in range(2):
            at = 2 * READ + direction * CROSS
            traces[at : at + CROSS] = cross_ref[direction]
        empty = 2 * READ + 2 * CROSS
        traces[empty] = jnp.zeros(traces.shape[1:], jnp.float32)
    if not last:
        cap = out_a.shape[0]
        acc[...] = jnp.zeros_like(acc)

    def entering(lane):
        if step:
            value = table_ref[RECV, lane]
            at = jnp.minimum(value & (SHIFT - 1), first_ref.shape[0] - 1)
            x = jnp.where(value < SHIFT, first_ref[at], second_ref[at])
            return x if step > 1 else jnp.where(value < 0, jnp.zeros_like(x), x)
        code = table_ref[CODE, lane]
        kind = lax.shift_right_logical(code, 1) & 3
        rdir = (kind ^ lax.shift_right_logical(kind, 1)) & 1
        group = lax.div(lax.shift_right_logical(code, 3) & 8191, tiles_dev)
        near = table_ref[SOURCE, lane]
        far = table_ref[FOREIGN, lane]
        near_at = jnp.where(near < 0, empty, jnp.where(rdir == odd, 0, READ) + near)
        far_at = jnp.where(far < 0, empty, 2 * READ + rdir * CROSS + far)
        at = jnp.where((group ^ place) < 2, near_at, far_at)
        return traces[jnp.clip(at, 0, empty)]

    def apply(lane, group, row, slot):
        real, imag = block_term(entering(lane), highs[group][row], lows[group][row])
        if slot is not None:
            if step == 0:
                total_ref[slot, 0] = real
                total_ref[slot, 1] = imag
            else:
                total_ref[slot, 0] += real
                total_ref[slot, 1] += imag
        if not last:
            value = table_ref[SEND, lane]
            at = jnp.where(value < SHIFT, value, value - SHIFT + cap)
            at = jnp.where(value < 0, 2 * cap, jnp.minimum(at, 2 * cap))
            acc[at, 0] += real
            acc[at, 1] += imag

    for group in range(2):
        base = (place ^ group) * STRIDE
        for j in range(LIVE):
            step_in = functools.partial(apply, base + j, group, j, group * LIVE + j)
            if step < 2:
                step_in()
            else:
                pl.when(table_ref[RECV, base + j] >= 0)(step_in)
    if not last:
        for group in range(2, 4):
            base = (place ^ group) * STRIDE
            for j in range(LIVE):
                rank = table_ref[COPY_IN, base + j]
                wanted = rank > 0
                if step:
                    wanted = wanted & (table_ref[RECV, base + j] >= 0)
                entry = jnp.clip(rank - 1, 0, EXTRA - 1)
                half = EXTRA // 2
                row = jnp.where(lax.div(entry, half) == core, 0, half) + lax.rem(entry, half)
                pl.when(wanted)(functools.partial(apply, base + j, 2, row, None))
        out_a[...] = acc[:cap]
        out_b[...] = acc[cap : 2 * cap]


def tick(step, tiles_dev, table, blocks, first, second, *data):
    sub = data[0].shape[-2]
    tile_shape = lambda count: jax.ShapeDtypeStruct((count, 2, sub, TILE), jnp.float32)
    room = lambda count: pltpu.VMEM((count, 2, sub, TILE), jnp.float32)
    out_shape = (tile_shape(2 * LIVE),)
    scratch = []
    aliases = {}
    if step == 0:
        scratch.append(room(2 * READ + 2 * CROSS + 1))
    else:
        aliases = {1 + len(blocks) + 2: 0}
    if step < len(ROUNDS):
        cap = ROUNDS[step]
        out_shape += (tile_shape(cap), tile_shape(cap))
        scratch.append(room(2 * cap + 1))
    operands = (*blocks, first, second, *data)
    return pl.pallas_call(
        functools.partial(tick_kernel, step, tiles_dev),
        out_shape=out_shape,
        in_specs=[SMEM] + [VMEM] * len(operands),
        out_specs=tuple(VMEM for _ in out_shape),
        scratch_shapes=scratch,
        input_output_aliases=aliases,
        compiler_params=PARAMS,
        name=f"tick_{step}",
    )(table, *operands)


def finish_kernel(share_ref, rows_ref, base_ref, total_ref, back_ref, out_ref, sums, sems):
    sub = back_ref.shape[2]
    core = share_ref[FACTS, 2] & 1
    short = share_ref[FACTS, 0] == 0

    def tile(j):
        return rows_ref[0, j], slice(None), slice(None), pl.ds(pl.multiple_of(rows_ref[1, j] * TILE, TILE), TILE)

    def move(source, target):
        copies = [pltpu.make_async_copy(source.at[tile(j)], target.at[tile(j)], sems.at[j]) for j in range(LIVE)]
        for copy in copies:
            copy.start()
        for copy in copies:
            copy.wait()

    move(base_ref, sums)
    for j in range(LIVE):
        direction, _, _, columns = tile(j)
        for flip, ref in enumerate((total_ref, back_ref)):
            shot = pl.multiple_of((core ^ flip) * sub, sub)
            for part in range(2):
                sums[direction, part, pl.ds(shot, sub), columns] += jnp.where(short, ref[j, part], 0.0)
    move(sums, out_ref)


def finish(share, rows, base, total, back):
    return pl.pallas_call(
        finish_kernel,
        out_shape=jax.ShapeDtypeStruct(base.shape, base.dtype),
        in_specs=[SMEM, SMEM, HBM, VMEM, VMEM],
        out_specs=HBM,
        scratch_shapes=[pltpu.VMEM(base.shape, base.dtype), pltpu.SemaphoreType.DMA((LIVE,))],
        input_output_aliases={2: 0},
        compiler_params=PARAMS,
        name="finish",
    )(share, rows, base, total, back)


def keep_sources(sources, green, rowcol, counts):
    return sources[0]


def body(sources, green, rowcol, counts):
    devices = lax.axis_size("tile")
    layers = lax.axis_size("layer")
    tiles_dev = sources.shape[-1] // TILE
    tiles = tiles_dev * devices
    if devices != 4 or 2 * tiles != 128 or tiles_dev != STRIDE:
        return full_sweeps(sources, green, rowcol, counts)[None]
    local = sources[0]
    where = jnp.stack([lax.axis_index("layer"), lax.axis_index("tile")]).astype(jnp.int32)

    codes, rows, order = slot_codes(where, rowcol[0], counts[0], layers * devices, 2 * tiles, tiles_dev)
    core, sub = lax.axis_index("tile") % 2, local.shape[2] // 2
    half_of = lambda which: lax.dynamic_slice_in_dim(local, which * sub, sub, axis=2)
    mine, theirs = half_of(core), swap_tile(half_of(1 - core), 1)
    table = lax.all_to_all(codes, ("layer", "tile"), 0, 0, tiled=True)
    packed, mine, theirs, table = lax.optimization_barrier((pack_green(order, green[0]), mine, theirs, table))
    picked = pick_tiles(where, table, mine, theirs, layers, devices, tiles_dev)
    picked, table = lax.optimization_barrier((picked, table))
    near = swap_layers(*picked)
    share, *steps = build_lists(where, table, layers, devices, tiles_dev)
    partner = swap_tile(packed, 1)
    copies = [swap_tile(block, 2) for block in lend_blocks(share, packed, partner)]
    shared, copies = lax.optimization_barrier((share_tiles(share, *near, tiles), copies))
    cross = swap_tile(shared, 2)
    copies = jnp.stack(copies)
    extra = split_green(jnp.concatenate([copies, swap_tile(copies, 1)]))
    highs, lows = zip(split_green(packed), split_green(partner), extra)
    blocks = highs + lows
    total, out_a, out_b = tick(0, tiles_dev, steps[0], blocks, *near, cross)
    out_a, out_b, sources = lax.optimization_barrier((out_a, out_b, sources))
    got = swap_layers(out_a, out_b)
    base = lax.cond(share[FACTS, 0] == 0, keep_sources, full_sweeps, sources, green, rowcol, counts)
    got, base = lax.optimization_barrier((got, base))
    for step in range(1, len(ROUNDS) + 1):
        total, *out = tick(step, tiles_dev, steps[step], blocks, *got, total)
        if out:
            got = swap_layers(*out)
    back = swap_tile(total[LIVE:], 1)
    out = finish(share, rows, base, total, back)
    return out[None]


def solution(mesh):
    return jax.shard_map(
        body,
        mesh=mesh,
        in_specs=(
            P("layer", None, None, None, "tile"),
            P("layer", "tile", None, None, None),
            P("layer", "tile", None),
            P("layer", "tile"),
        ),
        out_specs=P("layer", None, None, None, "tile"),
        check_vma=False,
    )
```
